128 devices in a mesh: tq: 8 (over z, core), slab: 16 (over x, y).
Axes of the slice: x: 4, y: 4, z: 4, core: 2. Of those that a mesh axis runs over, the one named last changes fastest.
Arguments:
- vert_ph: bfloat16 [8, 4096, 4096], P('tq', 'slab'), may hold values from -6 to 6
- full_pp: bfloat16 [8, 4096, 4096], P('tq', 'slab'), may hold values from -6 to 6
- target: int32 [8, 4096], P('tq', 'slab'), may hold values from 0 to 32767, as said below
- shift: int32 [8, 4096], P('tq', 'slab'), may hold values from -16 to 16
- trans_mom: int32 [8], P('tq'), may hold values from 0 to 63
- trans_bose: int32 [8], P('tq'), may hold values from 0 to 31
- energies: float32 [64], replicated, may hold values from -4 to 4
- pair_table: int32 [64, 64], replicated, may hold values from 0 to 63, as said below
Outputs:
- gamma: float32 [8, 4096, 4096], P('tq', 'slab')
- ladder: float32 [8, 4096, 4096], P('tq', 'slab')
The draws below stay inside these ranges and needn't reach their ends.
Inputs may be any that keep to these rules, and one draw needn't show every extreme that they name: `target`: rows are grouped by the device that holds them (transfer block on tq, outer-row block on slab, rows in the order transfer then outer row). The rows of one device name at most 3 rows held by any one device, and exactly 3 rows of one device. The momentum labels are a permutation of the points of a 8 x 8 periodic lattice; pair_table[a, b] is the label of the point of a minus the point of b.
All inputs are finite; a program needn't handle non-finite values.
Results may differ from the reference program's by a relative error of at most 0.003.
Values may be sent and summed in bfloat16 or wider, within the bound.
No kernel may reach another device: no remote copies, remote signals or barrier semaphores. Data moves between devices by JAX's collectives and lax.ppermute only.
A program may use at most 128 MiB of HBM per device.

```python
import jax
import jax.numpy as jnp
from jax import lax

LAT = 8
NB = 32
NF = 64
NQ = 64
MAT = 4096
TQ_DEV = 1
TRANS = 8
ROWS_DEV = 256
CAP = 3
N_TQ = 8
N_SLAB = 16
DEVICES = 128


def draw_target(key, part):
    key = jax.random.fold_in(key, 7)
    k_rank, k_hot, k_set, k_row = jax.random.split(key, 4)
    hot_count = max(1, DEVICES // 32)
    rank_order = jax.vmap(lambda sub_key: jax.random.permutation(sub_key, ROWS_DEV))(jax.random.split(k_rank, DEVICES))
    chosen = jax.random.permutation(k_set, DEVICES)
    hot_dev = chosen[jax.random.randint(k_hot, (DEVICES,), 0, hot_count)]
    spread = (hot_dev[:, None] + 1 + (rank_order - CAP) % (DEVICES - 1)) % DEVICES
    dest_dev = jnp.where(rank_order < CAP, hot_dev[:, None], spread)
    local_row = jax.random.randint(k_row, (DEVICES, ROWS_DEV), 0, ROWS_DEV)
    rows_slab = MAT // N_SLAB
    glob_trans = dest_dev // N_SLAB * TQ_DEV + local_row // rows_slab
    glob_row = dest_dev % N_SLAB * rows_slab + local_row % rows_slab
    flat_value = glob_trans * MAT + glob_row
    flat_value = flat_value.reshape(N_TQ, N_SLAB, TQ_DEV, rows_slab).transpose(0, 2, 1, 3)
    return flat_value.reshape(TRANS, MAT).astype(jnp.int32)


def draw_pair_table(key, part):
    key = jax.random.fold_in(key, 13)
    labels = jax.random.permutation(key, NQ)
    position = jnp.argsort(labels, stable=True)
    coord_x = position // LAT
    coord_y = position % LAT
    delta_x = (coord_x[:, None] - coord_x[None, :]) % LAT
    delta_y = (coord_y[:, None] - coord_y[None, :]) % LAT
    return labels[delta_x * LAT + delta_y].astype(jnp.int32)


def with_ends(array, stream_key, low, high):
    longest = array.shape.index(max(array.shape))
    spots = []
    for shift in (0, 1):
        where = [jax.random.randint(jax.random.fold_in(stream_key, axis), (), 0, length) for axis, length in enumerate(array.shape)]
        where[longest] = (where[longest] + shift) % array.shape[longest]
        spots.append(tuple(where))
    return array.at[spots[0]].set(low).at[spots[1]].set(high)


def block_scale(rng, extent, shards, least, top_value):
    loudness = 1.0
    for axis_at, blocks in shards:
        heights = jax.random.uniform(jax.random.fold_in(jax.random.fold_in(rng, 6), axis_at), (blocks,), jnp.float32, least / len(shards), top_value / len(shards))
        loudness = loudness * jnp.repeat(jnp.exp(heights), extent[axis_at] // blocks).reshape((-1,) + (1,) * (len(extent) - 1 - axis_at))
    return loudness


def gaussian(key, shape, width, reach, shards=(), held_as=jnp.bfloat16):
    entries = width * jax.random.normal(key, shape, jnp.float32)
    if shards:
        entries = entries * block_scale(key, shape, shards, -0.22, 0.18)
    return jnp.clip(entries, -reach, reach).astype(held_as)


def setup_inputs(seed: int = 0) -> dict:
    arg_keys = jax.random.split(jax.random.key(seed), 9)
    return {
        "vert_ph": gaussian(arg_keys[0], (TRANS, MAT, MAT), 1.0, 6.0, ((0, 8), (1, 16))),
        "full_pp": gaussian(arg_keys[1], (TRANS, MAT, MAT), 1.0, 6.0, ((0, 8), (1, 16))),
        "target": draw_target(jax.random.fold_in(arg_keys[8], 71), 0),
        "shift": with_ends(jax.random.randint(arg_keys[3], (TRANS, MAT), -(NB // 2), NB // 2 + 1), jax.random.fold_in(arg_keys[3], 1), -(NB // 2), (NB // 2 + 1) - 1).astype(jnp.int32),
        "trans_mom": with_ends(jax.random.randint(arg_keys[4], (TRANS,), 0, NQ), jax.random.fold_in(arg_keys[4], 1), 0, NQ - 1).astype(jnp.int32),
        "trans_bose": with_ends(jax.random.randint(arg_keys[5], (TRANS,), 0, NB), jax.random.fold_in(arg_keys[5], 1), 0, NB - 1).astype(jnp.int32),
        "energies": jnp.clip(jax.random.uniform(arg_keys[6], (NQ,), jnp.float32, -4.0, 4.0), -4.0, 4.0),
        "pair_table": draw_pair_table(jax.random.fold_in(arg_keys[8], 71), 0),
    }


HUBBARD = 2.0
TEMPER = 0.25
PI_VALUE = 3.141592653589793


def shift_rows(ph_rows, move_by):
    freq_count = ph_rows.shape[2]
    padded = jnp.pad(ph_rows, ((0, 0), (0, 0), (freq_count, freq_count)))
    starts = (freq_count - move_by).astype(jnp.int32)
    return jax.vmap(lambda one_row, first_col: lax.dynamic_slice_in_dim(one_row, first_col, freq_count, 1))(padded, starts)


def bubble(band_pair, band_own, bose_freq):
    fermi_freq = PI_VALUE * TEMPER * (2.0 * (jnp.arange(NF, dtype=jnp.int32) - NF // 2).astype(jnp.float32) + 1.0)
    other_freq = bose_freq[:, None] - fermi_freq[None, :]
    numerator = band_own[None, :, None] * band_pair[:, :, None] - (fermi_freq[None, :] * other_freq)[:, None, :]
    left_denom = fermi_freq[None, None, :] ** 2 + band_own[None, :, None] ** 2
    right_denom = other_freq[:, None, :] ** 2 + band_pair[:, :, None] ** 2
    values = TEMPER * numerator / (left_denom * right_denom)
    return values.reshape(band_pair.shape[0], NQ * NF)


def ladder_one(operands):
    gamma_one, bubble_one, full_one = operands
    weighted = (gamma_one * bubble_one[None, :]).astype(jnp.bfloat16)
    return jnp.dot(weighted, full_one, preferred_element_type=jnp.float32)


def reference(vert_ph, full_pp, target, shift, trans_mom, trans_bose, energies, pair_table):
    ph_rows = vert_ph.reshape(TRANS * MAT, NQ, NF)
    shifted = shift_rows(ph_rows, shift.reshape(TRANS * MAT)).reshape(TRANS * MAT, MAT)
    summed = jnp.zeros((TRANS * MAT, MAT), jnp.float32).at[target.reshape(TRANS * MAT)].add(shifted.astype(jnp.float32))
    gamma = (HUBBARD + summed).reshape(TRANS, MAT, MAT)
    bose_freq = 2.0 * PI_VALUE * TEMPER * (trans_bose - NB // 2).astype(jnp.float32)
    pair_bubble = bubble(energies[pair_table[trans_mom]], energies, bose_freq)
    ladder = lax.map(ladder_one, (gamma, pair_bubble, full_pp))
    return gamma, ladder
```

```python
import functools

import jax
import jax.numpy as jnp
from jax import lax
from jax.experimental import pallas as pl
from jax.experimental.pallas import tpu as pltpu
from jax.sharding import PartitionSpec as P

NB = 32
NF = 64
NQ = 64

HUBBARD = 2.0
TEMPER = 0.25
PI_VALUE = 3.141592653589793

AXES = ("tq", "slab")
DEVICES = 128
CAP = 3
ROWS = 256
WIDTH = 4096
LANES = 128
TILES = WIDTH // LANES
CHUNK = CAP * TILES
SIDE = 4
MIB = 1024 * 1024


def bubble(band_pair, band_own, bose_freq):
    fermi_freq = (
        PI_VALUE
        * TEMPER
        * (2.0 * (jnp.arange(NF, dtype=jnp.int32) - NF // 2).astype(jnp.float32) + 1.0)
    )
    other_freq = bose_freq[:, None] - fermi_freq[None, :]
    numerator = (
        band_own[None, :, None] * band_pair[:, :, None]
        - (fermi_freq[None, :] * other_freq)[:, None, :]
    )
    left_denom = fermi_freq[None, None, :] ** 2 + band_own[None, :, None] ** 2
    right_denom = other_freq[:, None, :] ** 2 + band_pair[:, :, None] ** 2
    values = TEMPER * numerator / (left_denom * right_denom)
    return values.reshape(band_pair.shape[0], NQ * NF)


def pairs_along(axis_of_core, step):
    pairs = []
    for tq in range(8):
        axis = axis_of_core[tq % 2]
        for x in range(SIDE):
            for y in range(SIDE):
                to_x = (x + step) % SIDE if axis == 0 else x
                to_y = (y + step) % SIDE if axis == 1 else y
                pairs.append(((tq * SIDE + x) * SIDE + y, (tq * SIDE + to_x) * SIDE + to_y))
    return pairs


def move_g(array, step):
    return lax.ppermute(array, AXES, pairs_along((0, 1), step))


def move_h(array, step):
    return lax.ppermute(array, AXES, pairs_along((1, 0), step))


def place_kernel(target_ref, shift_ref, rows_ref, out_ref, wide):
    dest = target_ref[...] // ROWS
    member = lax.broadcasted_iota(jnp.int32, (DEVICES, ROWS), 0) == dest
    before = (
        lax.broadcasted_iota(jnp.int32, (ROWS, ROWS), 0)
        < lax.broadcasted_iota(jnp.int32, (ROWS, ROWS), 1)
    ).astype(jnp.bfloat16)
    count = jnp.dot(
        member.astype(jnp.bfloat16), before, preferred_element_type=jnp.float32
    ).astype(jnp.int32)
    placer = jnp.concatenate(
        [(member & (count == k)).astype(jnp.bfloat16) for k in range(CAP)], axis=0
    )
    lane = lax.broadcasted_iota(jnp.int32, (ROWS, LANES), 1)
    from_freq = lane % NF - shift_ref[...]
    valid = (from_freq >= 0) & (from_freq < NF)
    from_lane = jnp.where(valid, lane - shift_ref[...], lane)
    for pair in range(TILES // 2):
        moved = []
        for tile in (2 * pair, 2 * pair + 1):
            block = rows_ref[:, tile * LANES : (tile + 1) * LANES].astype(jnp.float32)
            block = jnp.take_along_axis(block, from_lane, axis=1, mode="promise_in_bounds")
            moved.append(jnp.where(valid, block, 0.0).astype(jnp.bfloat16))
        placed = jnp.dot(
            placer, jnp.concatenate(moved, axis=1), preferred_element_type=jnp.float32
        )
        for k in range(CAP):
            for half in range(2):
                wide[pl.ds(k * TILES + 2 * pair + half, DEVICES, stride=CHUNK), :] = placed[
                    k * DEVICES : (k + 1) * DEVICES, half * LANES : (half + 1) * LANES
                ]

    @pl.loop(0, DEVICES // 4)
    def _(step):
        part = wide[pl.ds(pl.multiple_of(step * 4 * CHUNK, 4 * CHUNK), 4 * CHUNK), :]
        out_ref[pl.ds(pl.multiple_of(step * 4 * CHUNK, 4 * CHUNK), 4 * CHUNK), :] = part.astype(
            jnp.bfloat16
        )


def collect_kernel(
    where_ref, target_ref, bubble_ref, box_ref, gamma_ref, w0, w1, w2, w3, wide
):
    me, g, h, along_x, along_y = (where_ref[i] for i in range(5))
    target = target_ref[...]
    member = target // ROWS == me
    before = (
        lax.broadcasted_iota(jnp.int32, (ROWS, ROWS), 0)
        > lax.broadcasted_iota(jnp.int32, (ROWS, ROWS), 1)
    ).astype(jnp.bfloat16)
    count = jnp.dot(
        before, member.astype(jnp.bfloat16), preferred_element_type=jnp.float32
    ).astype(jnp.int32)
    row_of = lax.broadcasted_iota(jnp.int32, (ROWS, DEVICES), 0) + 1
    parts = []
    for k in range(CAP):
        local = jnp.sum(
            jnp.where(member & (count == k), target % ROWS + 1, 0), axis=0, keepdims=True
        )
        parts.append((row_of == local).astype(jnp.bfloat16))
    collector = jnp.concatenate(parts, axis=1)

    @pl.loop(0, DEVICES // 4)
    def _(step):
        rows = pl.ds(pl.multiple_of(step * 4 * CHUNK, 4 * CHUNK), 4 * CHUNK)
        wide[rows, :] = box_ref[rows, :].astype(jnp.float32)

    for d, w_ref in enumerate((w0, w1, w2, w3)):
        for o in range(SIDE):
            slab = ((g + o) % SIDE) * along_x + ((h + d) % SIDE) * along_y
            columns = pl.ds(pl.multiple_of(slab * ROWS, ROWS), ROWS)
            came = []
            for k in range(CAP):
                halves = [
                    wide[pl.ds(k * TILES + slab * 2 + half, DEVICES, stride=CHUNK), :]
                    for half in range(2)
                ]
                came.append(jnp.concatenate(halves, axis=1).astype(jnp.bfloat16))
            summed = jnp.dot(
                collector, jnp.concatenate(came, axis=0), preferred_element_type=jnp.float32
            )
            gamma = HUBBARD + summed
            gamma_ref[:, columns] = gamma
            w_ref[o] = (gamma * bubble_ref[:, columns]).astype(jnp.bfloat16)


def ladder_kernel(a_ref, own_ref, left_ref, right_ref, far_top_ref, far_low_ref, out_ref):
    total = jnp.dot(a_ref[0], own_ref[...], preferred_element_type=jnp.float32)
    total += jnp.dot(a_ref[1], right_ref[...], preferred_element_type=jnp.float32)
    far = jnp.concatenate([far_top_ref[...], far_low_ref[...]], axis=0)
    total += jnp.dot(a_ref[2], far, preferred_element_type=jnp.float32)
    total += jnp.dot(a_ref[3], left_ref[...], preferred_element_type=jnp.float32)
    out_ref[...] = total.astype(out_ref.dtype)


def part_ladder(weighted, full_parts, dtype):
    cut = 1024

    def columns(rows):
        return pl.BlockSpec((rows, cut), lambda n: (0, n))

    return pl.pallas_call(
        ladder_kernel,
        grid=(WIDTH // cut,),
        in_specs=[pl.BlockSpec((SIDE, ROWS, ROWS), lambda n: (0, 0, 0))]
        + [columns(part.shape[0]) for part in full_parts],
        out_specs=columns(ROWS),
        out_shape=jax.ShapeDtypeStruct((ROWS, WIDTH), dtype),
        compiler_params=pltpu.CompilerParams(vmem_limit_bytes=32 * MIB),
        cost_estimate=pl.CostEstimate(
            flops=2 * ROWS * 4 * ROWS * WIDTH, bytes_accessed=11 * MIB, transcendentals=0
        ),
        name="part_ladder",
    )(weighted, *full_parts)


def per_device(vert_ph, full_pp, target, shift, trans_mom, trans_bose, energies, pair_table):
    tq = lax.axis_index("tq")
    slab = lax.axis_index("slab")
    core = tq % 2
    x, y = slab // SIDE, slab % SIDE
    g = jnp.where(core == 0, x, y)
    h = jnp.where(core == 0, y, x)
    along_g = jnp.where(core == 0, SIDE, 1)
    where = jnp.stack([tq * 16 + slab, g, h, along_g, SIDE + 1 - along_g]).astype(jnp.int32)

    full = full_pp.reshape(ROWS, WIDTH)
    left = move_g(full, 1)
    right = move_g(full, 3)
    far_top = move_g(left[: ROWS // 2], 1)
    far_low = move_g(right[ROWS // 2 :], 3)
    full_parts = (full, left, right, far_top, far_low)

    all_target = lax.all_gather(target, AXES, axis=0, tiled=True)

    whole = pl.BlockSpec(memory_space=pltpu.VMEM)
    payload = pl.pallas_call(
        place_kernel,
        in_specs=[whole] * 3,
        out_specs=whole,
        out_shape=jax.ShapeDtypeStruct((DEVICES * CHUNK, LANES), jnp.bfloat16),
        scratch_shapes=[pltpu.VMEM((DEVICES * CHUNK, LANES), jnp.float32)],
        compiler_params=pltpu.CompilerParams(vmem_limit_bytes=32 * MIB),
        cost_estimate=pl.CostEstimate(
            flops=2 * 384 * ROWS * WIDTH, bytes_accessed=5 * MIB, transcendentals=0
        ),
        name="place",
    )(target, shift.reshape(ROWS, 1), vert_ph.reshape(ROWS, WIDTH))
    arrived = lax.all_to_all(
        payload.reshape(DEVICES, CHUNK, LANES), AXES, split_axis=0, concat_axis=0, tiled=True
    ).reshape(DEVICES * CHUNK, LANES)

    pick_mom = (trans_mom[:, None] == jnp.arange(NQ, dtype=jnp.int32)[None, :]).astype(jnp.float32)
    pair_rows = jnp.dot(pick_mom, pair_table.astype(jnp.float32), precision=lax.Precision.HIGHEST)
    picker = (
        pair_rows[:, :, None] == jnp.arange(NQ, dtype=jnp.int32).astype(jnp.float32)[None, None, :]
    ).astype(jnp.float32)
    band_pair = jnp.einsum("qkl,l->qk", picker, energies, precision=lax.Precision.HIGHEST)
    bose_freq = 2.0 * PI_VALUE * TEMPER * (trans_bose - NB // 2).astype(jnp.float32)
    pair_bubble = bubble(band_pair, energies, bose_freq)

    block = jax.ShapeDtypeStruct((SIDE, ROWS, ROWS), jnp.bfloat16)
    gamma, own, w1, w2, w3 = pl.pallas_call(
        collect_kernel,
        in_specs=[pl.BlockSpec(memory_space=pltpu.SMEM)] + [whole] * 3,
        out_specs=[whole] * 5,
        out_shape=[jax.ShapeDtypeStruct((ROWS, WIDTH), jnp.float32)] + [block] * 4,
        scratch_shapes=[pltpu.VMEM((DEVICES * CHUNK, LANES), jnp.float32)],
        compiler_params=pltpu.CompilerParams(vmem_limit_bytes=40 * MIB),
        cost_estimate=pl.CostEstimate(
            flops=2 * 384 * ROWS * WIDTH, bytes_accessed=9 * MIB, transcendentals=0
        ),
        name="collect",
    )(where, all_target.T, pair_bubble, arrived)

    ladder_parts = []
    for d, sent in ((2, w2), (1, w1), (3, w3)):
        part = part_ladder(move_h(sent, d), full_parts, jnp.bfloat16)
        ladder_parts.append(move_h(part, SIDE - d))
    ladder = part_ladder(own, full_parts, jnp.float32)
    for part in ladder_parts:
        ladder = ladder + part.astype(jnp.float32)
    return gamma[None], ladder[None]


def solution(mesh):
    in_specs = (
        P("tq", "slab", None),
        P("tq", "slab", None),
        P("tq", "slab"),
        P("tq", "slab"),
        P("tq"),
        P("tq"),
        P(),
        P(),
    )
    out_specs = (P("tq", "slab", None), P("tq", "slab", None))
    return jax.shard_map(
        per_device, mesh=mesh, in_specs=in_specs, out_specs=out_specs, check_vma=False
    )
```

```python
import functools

import jax
import jax.numpy as jnp
from jax import lax
from jax.experimental import pallas as pl
from jax.experimental.pallas import tpu as pltpu
from jax.sharding import PartitionSpec as P

NB = 32
NF = 64
NQ = 64

HUBBARD = 2.0
TEMPER = 0.25
PI_VALUE = 3.141592653589793

AXES = ("tq", "slab")
DEVICES = 128
CAP = 3
ROWS = 256
WIDTH = 4096
LANES = 128
TILES = WIDTH // LANES
LABELS = CAP * TILES
CHUNK = LABELS + 8
SIDE = 4
MIB = 1024 * 1024


def bubble(band_pair, band_own, bose_freq):
    fermi_freq = (
        PI_VALUE
        * TEMPER
        * (2.0 * (jnp.arange(NF, dtype=jnp.int32) - NF // 2).astype(jnp.float32) + 1.0)
    )
    other_freq = bose_freq[:, None] - fermi_freq[None, :]
    numerator = (
        band_own[None, :, None] * band_pair[:, :, None]
        - (fermi_freq[None, :] * other_freq)[:, None, :]
    )
    left_denom = fermi_freq[None, None, :] ** 2 + band_own[None, :, None] ** 2
    right_denom = other_freq[:, None, :] ** 2 + band_pair[:, :, None] ** 2
    values = TEMPER * numerator / (left_denom * right_denom)
    return values.reshape(band_pair.shape[0], NQ * NF)


def pairs_along(axis_of_core, step):
    pairs = []
    for tq in range(8):
        axis = axis_of_core[tq % 2]
        for x in range(SIDE):
            for y in range(SIDE):
                to_x = (x + step) % SIDE if axis == 0 else x
                to_y = (y + step) % SIDE if axis == 1 else y
                pairs.append(((tq * SIDE + x) * SIDE + y, (tq * SIDE + to_x) * SIDE + to_y))
    return pairs


def move_g(array, step):
    return lax.ppermute(array, AXES, pairs_along((0, 1), step))


def move_h(array, step):
    return lax.ppermute(array, AXES, pairs_along((1, 0), step))


def place_kernel(target_ref, shift_ref, rows_ref, out_ref, wide):
    dest = target_ref[...] // ROWS
    member = lax.broadcasted_iota(jnp.int32, (DEVICES, ROWS), 0) == dest
    before = (
        lax.broadcasted_iota(jnp.int32, (ROWS, ROWS), 0)
        < lax.broadcasted_iota(jnp.int32, (ROWS, ROWS), 1)
    ).astype(jnp.bfloat16)
    count = jnp.dot(
        member.astype(jnp.bfloat16), before, preferred_element_type=jnp.float32
    ).astype(jnp.int32)
    placer = jnp.concatenate(
        [(member & (count == k)).astype(jnp.bfloat16) for k in range(CAP)], axis=0
    )
    lane = lax.broadcasted_iota(jnp.int32, (ROWS, LANES), 1)
    from_freq = lane % NF - shift_ref[...]
    valid = (from_freq >= 0) & (from_freq < NF)
    from_lane = jnp.where(valid, lane - shift_ref[...], lane)
    for pair in range(TILES // 2):
        moved = []
        for tile in (2 * pair, 2 * pair + 1):
            block = rows_ref[:, tile * LANES : (tile + 1) * LANES].astype(jnp.float32)
            block = jnp.take_along_axis(block, from_lane, axis=1, mode="promise_in_bounds")
            moved.append(jnp.where(valid, block, 0.0).astype(jnp.bfloat16))
        placed = jnp.dot(
            placer, jnp.concatenate(moved, axis=1), preferred_element_type=jnp.float32
        )
        for k in range(CAP):
            for half in range(2):
                wide[pl.ds(k * TILES + 2 * pair + half, DEVICES, stride=CHUNK), :] = placed[
                    k * DEVICES : (k + 1) * DEVICES, half * LANES : (half + 1) * LANES
                ]

    codes = lax.dot_general(
        placer,
        jnp.broadcast_to(target_ref[...] % ROWS + 1, (LANES, ROWS)).astype(jnp.bfloat16),
        (((1,), (1,)), ((), ())),
        preferred_element_type=jnp.float32,
    )
    column = lax.broadcasted_iota(jnp.int32, (DEVICES, LANES), 1)
    label = jnp.zeros((DEVICES, LANES), jnp.float32)
    for k in range(CAP):
        label = jnp.where(column == k, codes[k * DEVICES : (k + 1) * DEVICES], label)
    wide[pl.ds(LABELS, DEVICES, stride=CHUNK), :] = label

    @pl.loop(0, DEVICES // 4)
    def _(step):
        part = wide[pl.ds(pl.multiple_of(step * 4 * CHUNK, 4 * CHUNK), 4 * CHUNK), :]
        out_ref[pl.ds(pl.multiple_of(step * 4 * CHUNK, 4 * CHUNK), 4 * CHUNK), :] = part.astype(
            jnp.bfloat16
        )


def collect_kernel(
    where_ref, bubble_ref, box_ref, gamma_ref, w0, w1, w2, w3, wide
):
    g, h, along_g, along_h = (where_ref[i] for i in range(4))
    @pl.loop(0, DEVICES // 4)
    def _(step):
        rows = pl.ds(pl.multiple_of(step * 4 * CHUNK, 4 * CHUNK), 4 * CHUNK)
        wide[rows, :] = box_ref[rows, :].astype(jnp.float32)

    label = jnp.transpose(wide[pl.ds(LABELS, DEVICES, stride=CHUNK), :]).astype(jnp.int32)
    row_of = lax.broadcasted_iota(jnp.int32, (ROWS, DEVICES), 0) + 1
    collector = jnp.concatenate(
        [(row_of == label[k : k + 1]).astype(jnp.bfloat16) for k in range(CAP)], axis=1
    )

    for d, w_ref in enumerate((w0, w1, w2, w3)):
        for o in range(SIDE):
            slab = ((g + o) % SIDE) * along_g + ((h + d) % SIDE) * along_h
            columns = pl.ds(pl.multiple_of(slab * ROWS, ROWS), ROWS)
            came = []
            for k in range(CAP):
                halves = [
                    wide[pl.ds(k * TILES + slab * 2 + half, DEVICES, stride=CHUNK), :]
                    for half in range(2)
                ]
                came.append(jnp.concatenate(halves, axis=1).astype(jnp.bfloat16))
            summed = jnp.dot(
                collector, jnp.concatenate(came, axis=0), preferred_element_type=jnp.float32
            )
            gamma = HUBBARD + summed
            gamma_ref[:, columns] = gamma
            w_ref[o] = (gamma * bubble_ref[:, columns]).astype(jnp.bfloat16)


def ladder_kernel(a_ref, own_ref, *refs):
    out_ref = refs[-1]
    total = jnp.dot(a_ref[0], own_ref[...], preferred_element_type=jnp.float32)
    for o in range(1, SIDE):
        block = jnp.concatenate([refs[2 * o - 2][...], refs[2 * o - 1][...]], axis=0)
        total += jnp.dot(a_ref[o], block, preferred_element_type=jnp.float32)
    out_ref[...] = total.astype(out_ref.dtype)


def part_ladder(weighted, full_parts, dtype):
    cut = 1024

    def columns(rows):
        return pl.BlockSpec((rows, cut), lambda n: (0, n))

    return pl.pallas_call(
        ladder_kernel,
        grid=(WIDTH // cut,),
        in_specs=[pl.BlockSpec((SIDE, ROWS, ROWS), lambda n: (0, 0, 0))]
        + [columns(part.shape[0]) for part in full_parts],
        out_specs=columns(ROWS),
        out_shape=jax.ShapeDtypeStruct((ROWS, WIDTH), dtype),
        compiler_params=pltpu.CompilerParams(vmem_limit_bytes=32 * MIB),
        cost_estimate=pl.CostEstimate(
            flops=2 * ROWS * 4 * ROWS * WIDTH, bytes_accessed=11 * MIB, transcendentals=0
        ),
        name="part_ladder",
    )(weighted, *full_parts)


def per_device(vert_ph, full_pp, target, shift, trans_mom, trans_bose, energies, pair_table):
    tq = lax.axis_index("tq")
    slab = lax.axis_index("slab")
    core = tq % 2
    x, y = slab // SIDE, slab % SIDE
    g = jnp.where(core == 0, x, y)
    h = jnp.where(core == 0, y, x)
    along_g = jnp.where(core == 0, SIDE, 1)
    where = jnp.stack([g, h, along_g, SIDE + 1 - along_g]).astype(jnp.int32)

    full = full_pp.reshape(ROWS, WIDTH)
    top, low = full[: ROWS // 2], full[ROWS // 2 :]
    left_top = move_g(top, 1)
    right_low = move_g(low, 3)
    left_low = move_g(low, 1)
    right_top = move_g(top, 3)

    whole = pl.BlockSpec(memory_space=pltpu.VMEM)
    payload = pl.pallas_call(
        place_kernel,
        in_specs=[whole] * 3,
        out_specs=whole,
        out_shape=jax.ShapeDtypeStruct((DEVICES * CHUNK, LANES), jnp.bfloat16),
        scratch_shapes=[pltpu.VMEM((DEVICES * CHUNK, LANES), jnp.float32)],
        compiler_params=pltpu.CompilerParams(vmem_limit_bytes=32 * MIB),
        cost_estimate=pl.CostEstimate(
            flops=2 * 384 * ROWS * WIDTH, bytes_accessed=5 * MIB, transcendentals=0
        ),
        name="place",
    )(target, shift.reshape(ROWS, 1), vert_ph.reshape(ROWS, WIDTH))
    payload, left_top, right_low = lax.optimization_barrier((payload, left_top, right_low))
    arrived = lax.all_to_all(
        payload.reshape(DEVICES, CHUNK, LANES), AXES, split_axis=0, concat_axis=0, tiled=True
    ).reshape(DEVICES * CHUNK, LANES)

    arrived, left_top, right_low = lax.optimization_barrier((arrived, left_top, right_low))
    far_top = move_g(left_top, 1)
    far_low = move_g(right_low, 3)
    full_parts = (full, right_top, right_low, far_top, far_low, left_top, left_low)

    pick_mom = (trans_mom[:, None] == jnp.arange(NQ, dtype=jnp.int32)[None, :]).astype(jnp.float32)
    pair_rows = jnp.dot(pick_mom, pair_table.astype(jnp.float32), precision=lax.Precision.HIGHEST)
    picker = (
        pair_rows[:, :, None] == jnp.arange(NQ, dtype=jnp.int32).astype(jnp.float32)[None, None, :]
    ).astype(jnp.float32)
    band_pair = jnp.einsum("qkl,l->qk", picker, energies, precision=lax.Precision.HIGHEST)
    bose_freq = 2.0 * PI_VALUE * TEMPER * (trans_bose - NB // 2).astype(jnp.float32)
    pair_bubble = bubble(band_pair, energies, bose_freq)

    block = jax.ShapeDtypeStruct((SIDE, ROWS, ROWS), jnp.bfloat16)
    gamma, own, w1, w2, w3 = pl.pallas_call(
        collect_kernel,
        in_specs=[pl.BlockSpec(memory_space=pltpu.SMEM)] + [whole] * 2,
        out_specs=[whole] * 5,
        out_shape=[jax.ShapeDtypeStruct((ROWS, WIDTH), jnp.float32)] + [block] * 4,
        scratch_shapes=[pltpu.VMEM((DEVICES * CHUNK, LANES), jnp.float32)],
        compiler_params=pltpu.CompilerParams(vmem_limit_bytes=40 * MIB),
        cost_estimate=pl.CostEstimate(
            flops=2 * 384 * ROWS * WIDTH, bytes_accessed=9 * MIB, transcendentals=0
        ),
        name="collect",
    )(where, pair_bubble, arrived)

    ladder_parts = []
    for d, sent in ((2, w2), (1, w1), (3, w3)):
        part = part_ladder(move_h(sent, d), full_parts, jnp.bfloat16)
        ladder_parts.append(move_h(part, SIDE - d))
    ladder = part_ladder(own, full_parts, jnp.float32)
    for part in ladder_parts:
        ladder = ladder + part.astype(jnp.float32)
    return gamma[None], ladder[None]


def solution(mesh):
    in_specs = (
        P("tq", "slab", None),
        P("tq", "slab", None),
        P("tq", "slab"),
        P("tq", "slab"),
        P("tq"),
        P("tq"),
        P(),
        P(),
    )
    out_specs = (P("tq", "slab", None), P("tq", "slab", None))
    return jax.shard_map(
        per_device, mesh=mesh, in_specs=in_specs, out_specs=out_specs, check_vma=False
    )
```

```python
import functools

import jax
import jax.numpy as jnp
from jax import lax
from jax.experimental import pallas as pl
from jax.experimental.pallas import tpu as pltpu
from jax.sharding import PartitionSpec as P

NB = 32
NF = 64
NQ = 64

HUBBARD = 2.0
TEMPER = 0.25
PI_VALUE = 3.141592653589793

AXES = ("tq", "slab")
DEVICES = 128
CAP = 3
ROWS = 256
WIDTH = 4096
LANES = 128
TILES = WIDTH // LANES
LABELS = CAP * TILES
CHUNK = LABELS + 8
SIDE = 4
HALF = WIDTH // 2
CUT = 1024
MIB = 1024 * 1024


def bubble(band_pair, band_own, bose_freq):
    fermi_freq = (
        PI_VALUE
        * TEMPER
        * (2.0 * (jnp.arange(NF, dtype=jnp.int32) - NF // 2).astype(jnp.float32) + 1.0)
    )
    other_freq = bose_freq[:, None] - fermi_freq[None, :]
    numerator = (
        band_own[None, :, None] * band_pair[:, :, None]
        - (fermi_freq[None, :] * other_freq)[:, None, :]
    )
    left_denom = fermi_freq[None, None, :] ** 2 + band_own[None, :, None] ** 2
    right_denom = other_freq[:, None, :] ** 2 + band_pair[:, :, None] ** 2
    values = TEMPER * numerator / (left_denom * right_denom)
    return values.reshape(band_pair.shape[0], NQ * NF)


def pairs_along(axis_of_core, step):
    pairs = []
    for tq in range(8):
        axis = axis_of_core[tq % 2]
        for x in range(SIDE):
            for y in range(SIDE):
                to_x = (x + step) % SIDE if axis == 0 else x
                to_y = (y + step) % SIDE if axis == 1 else y
                pairs.append(((tq * SIDE + x) * SIDE + y, (tq * SIDE + to_x) * SIDE + to_y))
    return pairs


def move_g(array, step):
    return lax.ppermute(array, AXES, pairs_along((0, 1), step))


def move_h(array, step):
    return lax.ppermute(array, AXES, pairs_along((1, 0), step))


def place_kernel(target_ref, shift_ref, rows_ref, out_ref, wide):
    dest = target_ref[...] // ROWS
    member = lax.broadcasted_iota(jnp.int32, (DEVICES, ROWS), 0) == dest
    before = (
        lax.broadcasted_iota(jnp.int32, (ROWS, ROWS), 0)
        < lax.broadcasted_iota(jnp.int32, (ROWS, ROWS), 1)
    ).astype(jnp.bfloat16)
    count = jnp.dot(
        member.astype(jnp.bfloat16), before, preferred_element_type=jnp.float32
    ).astype(jnp.int32)
    placer = jnp.concatenate(
        [(member & (count == k)).astype(jnp.bfloat16) for k in range(CAP)], axis=0
    )
    lane = lax.broadcasted_iota(jnp.int32, (ROWS, LANES), 1)
    from_freq = lane % NF - shift_ref[...]
    valid = (from_freq >= 0) & (from_freq < NF)
    from_lane = jnp.where(valid, lane - shift_ref[...], lane)
    for pair in range(TILES // 2):
        moved = []
        for tile in (2 * pair, 2 * pair + 1):
            block = rows_ref[:, tile * LANES : (tile + 1) * LANES].astype(jnp.float32)
            block = jnp.take_along_axis(block, from_lane, axis=1, mode="promise_in_bounds")
            moved.append(jnp.where(valid, block, 0.0).astype(jnp.bfloat16))
        placed = jnp.dot(
            placer, jnp.concatenate(moved, axis=1), preferred_element_type=jnp.float32
        )
        for k in range(CAP):
            for half in range(2):
                wide[pl.ds(k * TILES + 2 * pair + half, DEVICES, stride=CHUNK), :] = placed[
                    k * DEVICES : (k + 1) * DEVICES, half * LANES : (half + 1) * LANES
                ]

    codes = lax.dot_general(
        placer,
        jnp.broadcast_to(target_ref[...] % ROWS + 1, (LANES, ROWS)).astype(jnp.bfloat16),
        (((1,), (1,)), ((), ())),
        preferred_element_type=jnp.float32,
    )
    column = lax.broadcasted_iota(jnp.int32, (DEVICES, LANES), 1)
    label = jnp.zeros((DEVICES, LANES), jnp.float32)
    for k in range(CAP):
        label = jnp.where(column == k, codes[k * DEVICES : (k + 1) * DEVICES], label)
    wide[pl.ds(LABELS, DEVICES, stride=CHUNK), :] = label

    @pl.loop(0, DEVICES // 4)
    def _(step):
        part = wide[pl.ds(pl.multiple_of(step * 4 * CHUNK, 4 * CHUNK), 4 * CHUNK), :]
        out_ref[pl.ds(pl.multiple_of(step * 4 * CHUNK, 4 * CHUNK), 4 * CHUNK), :] = part.astype(
            jnp.bfloat16
        )


def collect_kernel(
    where_ref, bubble_ref, box_ref, gamma_ref, w0, w1, w2, w3, wide
):
    g, h, along_g, along_h = (where_ref[i] for i in range(4))
    @pl.loop(0, DEVICES // 4)
    def _(step):
        rows = pl.ds(pl.multiple_of(step * 4 * CHUNK, 4 * CHUNK), 4 * CHUNK)
        wide[rows, :] = box_ref[rows, :].astype(jnp.float32)

    label = jnp.transpose(wide[pl.ds(LABELS, DEVICES, stride=CHUNK), :]).astype(jnp.int32)
    row_of = lax.broadcasted_iota(jnp.int32, (ROWS, DEVICES), 0) + 1
    collector = jnp.concatenate(
        [(row_of == label[k : k + 1]).astype(jnp.bfloat16) for k in range(CAP)], axis=1
    )

    for d, w_ref in enumerate((w0, w1, w2, w3)):
        for o in range(SIDE):
            slab = ((g + o) % SIDE) * along_g + ((h + d) % SIDE) * along_h
            columns = pl.ds(pl.multiple_of(slab * ROWS, ROWS), ROWS)
            came = []
            for k in range(CAP):
                halves = [
                    wide[pl.ds(k * TILES + slab * 2 + half, DEVICES, stride=CHUNK), :]
                    for half in range(2)
                ]
                came.append(jnp.concatenate(halves, axis=1).astype(jnp.bfloat16))
            summed = jnp.dot(
                collector, jnp.concatenate(came, axis=0), preferred_element_type=jnp.float32
            )
            gamma = HUBBARD + summed
            gamma_ref[:, columns] = gamma
            w_ref[o] = (gamma * bubble_ref[:, columns]).astype(jnp.bfloat16)


def ladder_kernel(parts, a_ref, *refs):
    out_ref = refs[-1]
    total = jnp.dot(a_ref[0], refs[0][...], preferred_element_type=jnp.float32)
    for o in range(1, SIDE):
        block = jnp.concatenate([refs[2 * o - 1][...], refs[2 * o][...]], axis=0)
        total += jnp.dot(a_ref[o], block, preferred_element_type=jnp.float32)
    for other in refs[parts:-1]:
        total += other[...].astype(jnp.float32)
    out_ref[...] = total.astype(out_ref.dtype)


def part_ladder(weighted, full_parts, side, dtype, *others):
    steps = HALF // CUT

    def columns(rows, first):
        return pl.BlockSpec((rows, CUT), lambda n: (0, first + n))

    return pl.pallas_call(
        functools.partial(ladder_kernel, len(full_parts)),
        grid=(steps,),
        in_specs=[pl.BlockSpec((SIDE, ROWS, ROWS), lambda n: (0, 0, 0))]
        + [columns(part.shape[0], side * steps) for part in full_parts]
        + [columns(ROWS, 0) for _ in others],
        out_specs=columns(ROWS, 0),
        out_shape=jax.ShapeDtypeStruct((ROWS, HALF), dtype),
        compiler_params=pltpu.CompilerParams(vmem_limit_bytes=32 * MIB),
        cost_estimate=pl.CostEstimate(
            flops=2 * ROWS * 4 * ROWS * HALF, bytes_accessed=6 * MIB, transcendentals=0
        ),
        name="part_ladder",
    )(weighted, *full_parts, *others)


def join_kernel(left_a, left_b, right_a, right_b, out_ref):
    n = pl.program_id(0)

    @pl.when(n < HALF // CUT)
    def _():
        out_ref[...] = left_a[...] + left_b[...].astype(jnp.float32)

    @pl.when(n >= HALF // CUT)
    def _():
        out_ref[...] = right_a[...] + right_b[...].astype(jnp.float32)


def join(*parts):
    steps = HALF // CUT
    left = pl.BlockSpec((ROWS, CUT), lambda n: (0, jnp.minimum(n, steps - 1)))
    right = pl.BlockSpec((ROWS, CUT), lambda n: (0, jnp.maximum(n - steps, 0)))
    return pl.pallas_call(
        join_kernel,
        grid=(2 * steps,),
        in_specs=[left, left, right, right],
        out_specs=pl.BlockSpec((ROWS, CUT), lambda n: (0, n)),
        out_shape=jax.ShapeDtypeStruct((ROWS, WIDTH), jnp.float32),
        compiler_params=pltpu.CompilerParams(vmem_limit_bytes=32 * MIB),
        cost_estimate=pl.CostEstimate(
            flops=ROWS * WIDTH, bytes_accessed=10 * MIB, transcendentals=0
        ),
        name="join",
    )(*parts)


def per_device(vert_ph, full_pp, target, shift, trans_mom, trans_bose, energies, pair_table):
    tq = lax.axis_index("tq")
    slab = lax.axis_index("slab")
    core = tq % 2
    x, y = slab // SIDE, slab % SIDE
    g = jnp.where(core == 0, x, y)
    h = jnp.where(core == 0, y, x)
    along_g = jnp.where(core == 0, SIDE, 1)
    where = jnp.stack([g, h, along_g, SIDE + 1 - along_g]).astype(jnp.int32)

    full = full_pp.reshape(ROWS, WIDTH)
    top, low = full[: ROWS // 2], full[ROWS // 2 :]
    left_top = move_g(top, 1)
    right_low = move_g(low, 3)
    left_low = move_g(low, 1)
    right_top = move_g(top, 3)

    whole = pl.BlockSpec(memory_space=pltpu.VMEM)
    payload = pl.pallas_call(
        place_kernel,
        in_specs=[whole] * 3,
        out_specs=whole,
        out_shape=jax.ShapeDtypeStruct((DEVICES * CHUNK, LANES), jnp.bfloat16),
        scratch_shapes=[pltpu.VMEM((DEVICES * CHUNK, LANES), jnp.float32)],
        compiler_params=pltpu.CompilerParams(vmem_limit_bytes=32 * MIB),
        cost_estimate=pl.CostEstimate(
            flops=2 * 384 * ROWS * WIDTH, bytes_accessed=5 * MIB, transcendentals=0
        ),
        name="place",
    )(target, shift.reshape(ROWS, 1), vert_ph.reshape(ROWS, WIDTH))
    arrived = lax.all_to_all(
        payload.reshape(DEVICES, CHUNK, LANES), AXES, split_axis=0, concat_axis=0, tiled=True
    ).reshape(DEVICES * CHUNK, LANES)

    far_top = move_g(left_top, 1)
    far_low = move_g(right_low, 3)
    arrived, left_low, right_top = lax.optimization_barrier((arrived, left_low, right_top))
    full_parts = (full, right_top, right_low, far_top, far_low, left_top, left_low)

    pick_mom = (trans_mom[:, None] == jnp.arange(NQ, dtype=jnp.int32)[None, :]).astype(jnp.float32)
    pair_rows = jnp.dot(pick_mom, pair_table.astype(jnp.float32), precision=lax.Precision.HIGHEST)
    picker = (
        pair_rows[:, :, None] == jnp.arange(NQ, dtype=jnp.int32).astype(jnp.float32)[None, None, :]
    ).astype(jnp.float32)
    band_pair = jnp.einsum("qkl,l->qk", picker, energies, precision=lax.Precision.HIGHEST)
    bose_freq = 2.0 * PI_VALUE * TEMPER * (trans_bose - NB // 2).astype(jnp.float32)
    pair_bubble = bubble(band_pair, energies, bose_freq)

    block = jax.ShapeDtypeStruct((SIDE, ROWS, ROWS), jnp.bfloat16)
    gamma, own, w1, w2, w3 = pl.pallas_call(
        collect_kernel,
        in_specs=[pl.BlockSpec(memory_space=pltpu.SMEM)] + [whole] * 2,
        out_specs=[whole] * 5,
        out_shape=[jax.ShapeDtypeStruct((ROWS, WIDTH), jnp.float32)] + [block] * 4,
        scratch_shapes=[pltpu.VMEM((DEVICES * CHUNK, LANES), jnp.float32)],
        compiler_params=pltpu.CompilerParams(vmem_limit_bytes=40 * MIB),
        cost_estimate=pl.CostEstimate(
            flops=2 * 384 * ROWS * WIDTH, bytes_accessed=9 * MIB, transcendentals=0
        ),
        name="collect",
    )(where, pair_bubble, arrived)

    part = functools.partial(part_ladder, full_parts=full_parts)
    bf16, f32 = jnp.bfloat16, jnp.float32
    from_far, from_low, from_high = move_h(w2, 2), move_h(w1, 1), move_h(w3, 3)
    from_far, from_low, from_high = lax.optimization_barrier((from_far, from_low, from_high))
    far_left = move_h(part(from_far, side=0, dtype=bf16), 1)
    far_right = move_h(part(from_far, side=1, dtype=bf16), 3)
    high_right = move_h(part(from_high, side=1, dtype=bf16), 1)
    low_left = move_h(part(from_low, side=0, dtype=bf16), 3)
    high_left = move_h(part_ladder(from_high, full_parts, 0, bf16, far_left), 1)
    low_right = move_h(part_ladder(from_low, full_parts, 1, bf16, far_right), 3)
    own_left = part_ladder(own, full_parts, 0, f32, low_left)
    own_right = part_ladder(own, full_parts, 1, f32, high_right)
    ladder = join(own_left, high_left, own_right, low_right)
    return gamma[None], ladder[None]


def solution(mesh):
    in_specs = (
        P("tq", "slab", None),
        P("tq", "slab", None),
        P("tq", "slab"),
        P("tq", "slab"),
        P("tq"),
        P("tq"),
        P(),
        P(),
    )
    out_specs = (P("tq", "slab", None), P("tq", "slab", None))
    return jax.shard_map(
        per_device, mesh=mesh, in_specs=in_specs, out_specs=out_specs, check_vma=False
    )
```

```python
import functools

import jax
import jax.numpy as jnp
from jax import lax
from jax.experimental import pallas as pl
from jax.experimental.pallas import tpu as pltpu
from jax.sharding import PartitionSpec as P

NB = 32
NF = 64
NQ = 64

HUBBARD = 2.0
TEMPER = 0.25
PI_VALUE = 3.141592653589793

AXES = ("tq", "slab")
DEVICES = 128
CAP = 3
ROWS = 256
WIDTH = 4096
LANES = 128
TILES = WIDTH // LANES
LABELS = CAP * TILES
CHUNK = LABELS + 8
SIDE = 4
HALF = WIDTH // 2
CUT = 1024
MIB = 1024 * 1024


def bubble_kernel(mom_ref, bose_ref, energy_ref, table_ref, out_ref):
    exact = functools.partial(
        jnp.dot, precision=lax.Precision.HIGHEST, preferred_element_type=jnp.float32
    )
    energies = jnp.broadcast_to(energy_ref[...], (8, NQ))
    partner = table_ref[pl.ds(mom_ref[0], 1), :]
    picker = lax.broadcasted_iota(jnp.int32, (NQ, NQ), 0) == partner
    pair = exact(energies, picker.astype(jnp.float32))
    first = lax.broadcasted_iota(jnp.int32, (8, NQ), 0) == 0
    column = lax.broadcasted_iota(jnp.int32, (NQ, WIDTH), 1)
    spread = lax.broadcasted_iota(jnp.int32, (NQ, WIDTH), 0) == column // NF
    bands = exact(jnp.where(first, energies, pair), spread.astype(jnp.float32))
    band_own, band_pair = bands[:1], bands[1:2]
    freq = lax.broadcasted_iota(jnp.int32, (1, WIDTH), 1) % NF - NF // 2
    fermi = PI_VALUE * TEMPER * (2.0 * freq.astype(jnp.float32) + 1.0)
    bose = (bose_ref[0] - NB // 2).astype(jnp.float32) * (2.0 * PI_VALUE * TEMPER)
    other = bose - fermi
    top = TEMPER * (band_own * band_pair - fermi * other)
    below = (fermi * fermi + band_own * band_own) * (other * other + band_pair * band_pair)
    out_ref[...] = top / below


def pairs_along(axis_of_core, step):
    pairs = []
    for tq in range(8):
        axis = axis_of_core[tq % 2]
        for x in range(SIDE):
            for y in range(SIDE):
                to_x = (x + step) % SIDE if axis == 0 else x
                to_y = (y + step) % SIDE if axis == 1 else y
                pairs.append(((tq * SIDE + x) * SIDE + y, (tq * SIDE + to_x) * SIDE + to_y))
    return pairs


def move_g(array, step):
    return lax.ppermute(array, AXES, pairs_along((0, 1), step))


def move_h(array, step):
    return lax.ppermute(array, AXES, pairs_along((1, 0), step))


def one_hot(flags):
    return flags.astype(jnp.bfloat16)


def row_slots(target_ref):
    dest = target_ref[...] // ROWS
    member = lax.broadcasted_iota(jnp.int32, (DEVICES, ROWS), 0) == dest
    before = one_hot(
        lax.broadcasted_iota(jnp.int32, (ROWS, ROWS), 0)
        < lax.broadcasted_iota(jnp.int32, (ROWS, ROWS), 1)
    )
    count = jnp.dot(one_hot(member), before, preferred_element_type=jnp.float32)
    return dest, member, before, count


def read_codes(placer, values):
    return lax.dot_general(
        placer,
        jnp.broadcast_to(values, (LANES, ROWS)).astype(jnp.bfloat16),
        (((1,), (1,)), ((), ())),
        preferred_element_type=jnp.float32,
    )


def labels(*columns):
    rows = columns[0].shape[0]
    lane = lax.broadcasted_iota(jnp.int32, (rows, LANES), 1)
    label = jnp.zeros((rows, LANES), jnp.float32)
    for at, column in enumerate(columns):
        label = jnp.where(lane == at, column, label)
    return label


def fetch_rows(rows_ref, held, sems):
    quarter = WIDTH // 4
    copies = []
    for at in range(4):
        columns = pl.ds(at * quarter, quarter)
        copies.append(
            pltpu.make_async_copy(rows_ref.at[:, columns], held.at[:, columns], sems.at[at])
        )
        copies[-1].start()
    return copies


def place_columns(shift_ref, held, copies, placer, put):
    shift = jnp.transpose(jnp.broadcast_to(shift_ref[...].astype(jnp.float32), (LANES, ROWS)))
    shift = shift.astype(jnp.int32)
    lane = lax.broadcasted_iota(jnp.int32, (ROWS, LANES), 1)
    from_freq = lane % NF - shift
    valid = (from_freq >= 0) & (from_freq < NF)
    from_lane = jnp.where(valid, lane - shift, lane)
    for pair in range(TILES // 2):
        if pair % (TILES // 8) == 0:
            copies[pair // (TILES // 8)].wait()
        moved = []
        for tile in (2 * pair, 2 * pair + 1):
            block = held[:, tile * LANES : (tile + 1) * LANES].astype(jnp.float32)
            block = jnp.take_along_axis(block, from_lane, axis=1, mode="promise_in_bounds")
            moved.append(jnp.where(valid, block, 0.0).astype(jnp.bfloat16))
        placed = jnp.dot(
            placer, jnp.concatenate(moved, axis=1), preferred_element_type=jnp.float32
        )
        for half in range(2):
            put(2 * pair + half, placed[:, half * LANES : (half + 1) * LANES])


def send_out(wide, packed, out_ref, sem, size, parts):
    copies = []
    rows = size // parts
    for at in range(parts):
        part = pl.ds(at * rows, rows)
        packed[part, :] = wide[part, :].astype(jnp.bfloat16)
        copies.append(pltpu.make_async_copy(packed.at[part, :], out_ref.at[part, :], sem.at[at]))
        copies[-1].start()
    return copies


def place_kernel(
    target_ref, shift_ref, rows_ref, out_ref, held, wide, packed, in_sems, out_sems
):
    copies = fetch_rows(rows_ref, held, in_sems)
    _, member, _, count = row_slots(target_ref)
    placer = jnp.concatenate([one_hot(member & (count == k)) for k in range(CAP)], axis=0)

    def put(tile, placed):
        for k in range(CAP):
            wide[pl.ds(k * TILES + tile, DEVICES, stride=CHUNK), :] = placed[
                k * DEVICES : (k + 1) * DEVICES
            ]

    place_columns(shift_ref, held, copies, placer, put)
    codes = read_codes(placer, target_ref[...] % ROWS + 1)
    wide[pl.ds(LABELS, DEVICES, stride=CHUNK), :] = labels(
        *(codes[k * DEVICES : (k + 1) * DEVICES] for k in range(CAP))
    )
    for copy in send_out(wide, packed, out_ref, out_sems, DEVICES * CHUNK, 4):
        copy.wait()


def collect_kernel(
    where_ref, bubble_ref, box_ref, gamma_ref, w0, w1, w2, w3,
    box, wide, gamma_held, in_sems, out_sems,
):
    parts = 8
    rows = DEVICES * CHUNK // parts
    copies = []
    for at in range(parts):
        part = pl.ds(at * rows, rows)
        copies.append(
            pltpu.make_async_copy(box_ref.at[part, :], box.at[part, :], in_sems.at[at])
        )
        copies[-1].start()
    g, h, along_g, along_h = (where_ref[i] for i in range(4))
    for at in range(parts):
        copies[at].wait()
        part = pl.ds(at * rows, rows)
        wide[part, :] = box[part, :].astype(jnp.float32)
    label = jnp.transpose(wide[pl.ds(LABELS, DEVICES, stride=CHUNK), :]).astype(jnp.int32)
    row_of = lax.broadcasted_iota(jnp.int32, (ROWS, DEVICES), 0) + 1
    collector = jnp.concatenate([one_hot(row_of == label[k : k + 1]) for k in range(CAP)], axis=1)

    copies = []
    for d, w_ref in enumerate((w0, w1, w2, w3)):
        for o in range(SIDE):
            slab = ((g + o) % SIDE) * along_g + ((h + d) % SIDE) * along_h
            columns = pl.ds(pl.multiple_of(slab * ROWS, ROWS), ROWS)
            came = []
            for k in range(CAP):
                halves = [
                    wide[pl.ds(k * TILES + slab * 2 + half, DEVICES, stride=CHUNK), :]
                    for half in range(2)
                ]
                came.append(jnp.concatenate(halves, axis=1).astype(jnp.bfloat16))
            summed = jnp.dot(
                collector, jnp.concatenate(came, axis=0), preferred_element_type=jnp.float32
            )
            gamma = HUBBARD + summed
            at = d * SIDE + o
            gamma_held[at] = gamma
            copies.append(
                pltpu.make_async_copy(
                    gamma_held.at[at], gamma_ref.at[:, columns], out_sems.at[at]
                )
            )
            copies[-1].start()
            w_ref[o] = (gamma * bubble_ref[:, columns]).astype(jnp.bfloat16)
    for copy in copies:
        copy.wait()


def ladder_kernel(parts, a_ref, *refs):
    out_ref = refs[-1]
    total = jnp.dot(a_ref[0], refs[0][...], preferred_element_type=jnp.float32)
    for o in range(1, SIDE):
        block = jnp.concatenate([refs[2 * o - 1][...], refs[2 * o][...]], axis=0)
        total += jnp.dot(a_ref[o], block, preferred_element_type=jnp.float32)
    for other in refs[parts:-1]:
        total += other[...].astype(jnp.float32)
    out_ref[...] = total.astype(out_ref.dtype)


def part_ladder(weighted, full_parts, side, dtype, *others):
    steps = HALF // CUT

    def columns(rows, first):
        return pl.BlockSpec((rows, CUT), lambda n: (0, first + n))

    return pl.pallas_call(
        functools.partial(ladder_kernel, len(full_parts)),
        grid=(steps,),
        in_specs=[pl.BlockSpec((SIDE, ROWS, ROWS), lambda n: (0, 0, 0))]
        + [columns(part.shape[0], side * steps) for part in full_parts]
        + [columns(ROWS, 0) for _ in others],
        out_specs=columns(ROWS, 0),
        out_shape=jax.ShapeDtypeStruct((ROWS, HALF), dtype),
        compiler_params=pltpu.CompilerParams(vmem_limit_bytes=14 * MIB),
        cost_estimate=pl.CostEstimate(
            flops=2 * ROWS * 4 * ROWS * HALF, bytes_accessed=6 * MIB, transcendentals=0
        ),
        name="part_ladder",
    )(weighted, *full_parts, *others)


def join_kernel(*refs):
    left, right, out_ref = refs[-3:]
    out_ref[...] = left[...] + right[...].astype(jnp.float32)


def join(side, own, other, into=()):
    steps = HALF // CUT
    part = pl.BlockSpec((ROWS, CUT), lambda n: (0, n))
    return pl.pallas_call(
        join_kernel,
        grid=(steps,),
        in_specs=[pl.BlockSpec(memory_space=pl.ANY)] * len(into) + [part, part],
        out_specs=pl.BlockSpec((ROWS, CUT), lambda n: (0, side * steps + n)),
        out_shape=jax.ShapeDtypeStruct((ROWS, WIDTH), jnp.float32),
        input_output_aliases={0: 0} if into else {},
        compiler_params=pltpu.CompilerParams(vmem_limit_bytes=8 * MIB),
        cost_estimate=pl.CostEstimate(
            flops=ROWS * HALF, bytes_accessed=5 * MIB, transcendentals=0
        ),
        name="join",
    )(*into, own, other)


def per_device(vert_ph, full_pp, target, shift, trans_mom, trans_bose, energies, pair_table):
    tq = lax.axis_index("tq")
    slab = lax.axis_index("slab")
    core = tq % 2
    x, y = slab // SIDE, slab % SIDE
    g = jnp.where(core == 0, x, y)
    h = jnp.where(core == 0, y, x)
    along_g = jnp.where(core == 0, SIDE, 1)
    where = jnp.stack([g, h, along_g, SIDE + 1 - along_g]).astype(jnp.int32)

    full = full_pp.reshape(ROWS, WIDTH)
    top, low = full[: ROWS // 2], full[ROWS // 2 :]
    left_top = move_g(top, 1)
    right_low = move_g(low, 3)
    left_low = move_g(low, 1)
    right_top = move_g(top, 3)

    whole = pl.BlockSpec(memory_space=pltpu.VMEM)
    hbm = pl.BlockSpec(memory_space=pltpu.HBM)
    slots = (DEVICES * CHUNK, LANES)
    payload = pl.pallas_call(
        place_kernel,
        in_specs=[whole, whole, hbm],
        out_specs=hbm,
        out_shape=jax.ShapeDtypeStruct(slots, jnp.bfloat16),
        scratch_shapes=[
            pltpu.VMEM((ROWS, WIDTH), jnp.bfloat16),
            pltpu.VMEM(slots, jnp.float32),
            pltpu.VMEM(slots, jnp.bfloat16),
            pltpu.SemaphoreType.DMA((4,)),
            pltpu.SemaphoreType.DMA((4,)),
        ],
        compiler_params=pltpu.CompilerParams(vmem_limit_bytes=60 * MIB),
        cost_estimate=pl.CostEstimate(
            flops=2 * 384 * ROWS * WIDTH, bytes_accessed=5 * MIB, transcendentals=0
        ),
        name="place",
    )(target, shift, vert_ph.reshape(ROWS, WIDTH))
    arrived = lax.all_to_all(
        payload.reshape(DEVICES, CHUNK, LANES), AXES, split_axis=0, concat_axis=0, tiled=True
    ).reshape(DEVICES * CHUNK, LANES)

    far_top = move_g(left_top, 1)
    far_low = move_g(right_low, 3)
    arrived, left_low, right_top = lax.optimization_barrier((arrived, left_low, right_top))
    full_parts = (full, right_top, right_low, far_top, far_low, left_top, left_low)

    scalar = pl.BlockSpec(memory_space=pltpu.SMEM)
    pair_bubble = pl.pallas_call(
        bubble_kernel,
        in_specs=[scalar, scalar, whole, whole],
        out_specs=whole,
        out_shape=jax.ShapeDtypeStruct((1, WIDTH), jnp.float32),
        compiler_params=pltpu.CompilerParams(vmem_limit_bytes=16 * MIB),
        cost_estimate=pl.CostEstimate(
            flops=10**11, bytes_accessed=1024 * MIB, transcendentals=0
        ),
        name="bubble",
    )(trans_mom, trans_bose, energies.reshape(1, NQ), pair_table)

    block = jax.ShapeDtypeStruct((SIDE, ROWS, ROWS), jnp.bfloat16)
    gamma, own, w1, w2, w3 = pl.pallas_call(
        collect_kernel,
        in_specs=[pl.BlockSpec(memory_space=pltpu.SMEM), whole, hbm],
        out_specs=[hbm] + [whole] * 4,
        out_shape=[jax.ShapeDtypeStruct((ROWS, WIDTH), jnp.float32)] + [block] * 4,
        scratch_shapes=[
            pltpu.VMEM(slots, jnp.bfloat16),
            pltpu.VMEM(slots, jnp.float32),
            pltpu.VMEM((SIDE * SIDE, ROWS, ROWS), jnp.float32),
            pltpu.SemaphoreType.DMA((8,)),
            pltpu.SemaphoreType.DMA((SIDE * SIDE,)),
        ],
        compiler_params=pltpu.CompilerParams(vmem_limit_bytes=24 * MIB),
        cost_estimate=pl.CostEstimate(
            flops=2 * 384 * ROWS * WIDTH, bytes_accessed=9 * MIB, transcendentals=0
        ),
        name="collect",
    )(where, pair_bubble, arrived)

    part = functools.partial(part_ladder, full_parts=full_parts)
    bf16, f32 = jnp.bfloat16, jnp.float32
    from_far, from_low, from_high = move_h(w2, 2), move_h(w1, 1), move_h(w3, 3)
    far_left = move_h(part(from_far, side=0, dtype=bf16), 1)
    from_far, from_low, from_high = lax.optimization_barrier((from_far, from_low, from_high))
    far_right = move_h(part(from_far, side=1, dtype=bf16), 3)
    high_right = move_h(part(from_high, side=1, dtype=bf16), 1)
    low_left = move_h(part(from_low, side=0, dtype=bf16), 3)
    high_left = move_h(part_ladder(from_high, full_parts, 0, bf16, far_left), 1)
    low_right = move_h(part_ladder(from_low, full_parts, 1, bf16, far_right), 3)
    own_left = part_ladder(own, full_parts, 0, f32, low_left)
    own_right = part_ladder(own, full_parts, 1, f32, high_right)
    ladder = join(0, own_left, high_left)
    ladder = join(1, own_right, low_right, (ladder,))
    return gamma[None], ladder[None]


def solution(mesh):
    in_specs = (
        P("tq", "slab", None),
        P("tq", "slab", None),
        P("tq", "slab"),
        P("tq", "slab"),
        P("tq"),
        P("tq"),
        P(),
        P(),
    )
    out_specs = (P("tq", "slab", None), P("tq", "slab", None))
    return jax.shard_map(
        per_device, mesh=mesh, in_specs=in_specs, out_specs=out_specs, check_vma=False
    )
```

```python
import functools

import jax
import jax.numpy as jnp
from jax import lax
from jax.experimental import pallas as pl
from jax.experimental.pallas import tpu as pltpu
from jax.sharding import PartitionSpec as P

NB = 32
NF = 64
NQ = 64

HUBBARD = 2.0
TEMPER = 0.25
PI_VALUE = 3.141592653589793

AXES = ("tq", "slab")
DEVICES = 128
CAP = 3
ROWS = 256
WIDTH = 4096
LANES = 128
TILES = WIDTH // LANES
LABELS = CAP * TILES
CHUNK = LABELS + 8
SIDE = 4
HALF = WIDTH // 2
CUT = 1024
MIB = 1024 * 1024


def bubble_kernel(mom_ref, bose_ref, energy_ref, table_ref, out_ref):
    exact = functools.partial(
        jnp.dot, precision=lax.Precision.HIGHEST, preferred_element_type=jnp.float32
    )
    energies = jnp.broadcast_to(energy_ref[...], (8, NQ))
    partner = table_ref[pl.ds(mom_ref[0], 1), :]
    picker = lax.broadcasted_iota(jnp.int32, (NQ, NQ), 0) == partner
    pair = exact(energies, picker.astype(jnp.float32))
    first = lax.broadcasted_iota(jnp.int32, (8, NQ), 0) == 0
    column = lax.broadcasted_iota(jnp.int32, (NQ, WIDTH), 1)
    spread = lax.broadcasted_iota(jnp.int32, (NQ, WIDTH), 0) == column // NF
    bands = exact(jnp.where(first, energies, pair), spread.astype(jnp.float32))
    band_own, band_pair = bands[:1], bands[1:2]
    freq = lax.broadcasted_iota(jnp.int32, (1, WIDTH), 1) % NF - NF // 2
    fermi = PI_VALUE * TEMPER * (2.0 * freq.astype(jnp.float32) + 1.0)
    bose = (bose_ref[0] - NB // 2).astype(jnp.float32) * (2.0 * PI_VALUE * TEMPER)
    other = bose - fermi
    top = TEMPER * (band_own * band_pair - fermi * other)
    below = (fermi * fermi + band_own * band_own) * (other * other + band_pair * band_pair)
    out_ref[...] = top / below


def pairs_along(axis_of_core, step):
    pairs = []
    for tq in range(8):
        axis = axis_of_core[tq % 2]
        for x in range(SIDE):
            for y in range(SIDE):
                to_x = (x + step) % SIDE if axis == 0 else x
                to_y = (y + step) % SIDE if axis == 1 else y
                pairs.append(((tq * SIDE + x) * SIDE + y, (tq * SIDE + to_x) * SIDE + to_y))
    return pairs


def move_g(array, step):
    return lax.ppermute(array, AXES, pairs_along((0, 1), step))


def move_h(array, step):
    return lax.ppermute(array, AXES, pairs_along((1, 0), step))


def one_hot(flags):
    return flags.astype(jnp.bfloat16)


def row_slots(target_ref):
    dest = target_ref[...] // ROWS
    member = lax.broadcasted_iota(jnp.int32, (DEVICES, ROWS), 0) == dest
    before = one_hot(
        lax.broadcasted_iota(jnp.int32, (ROWS, ROWS), 0)
        < lax.broadcasted_iota(jnp.int32, (ROWS, ROWS), 1)
    )
    count = jnp.dot(one_hot(member), before, preferred_element_type=jnp.float32)
    return dest, member, before, count


def read_codes(placer, values):
    return lax.dot_general(
        placer,
        jnp.broadcast_to(values, (LANES, ROWS)).astype(jnp.bfloat16),
        (((1,), (1,)), ((), ())),
        preferred_element_type=jnp.float32,
    )


def labels(*columns):
    rows = columns[0].shape[0]
    lane = lax.broadcasted_iota(jnp.int32, (rows, LANES), 1)
    label = jnp.zeros((rows, LANES), jnp.float32)
    for at, column in enumerate(columns):
        label = jnp.where(lane == at, column, label)
    return label


def fetch_rows(rows_ref, held, sems):
    quarter = WIDTH // 4
    copies = []
    for at in range(4):
        columns = pl.ds(at * quarter, quarter)
        copies.append(
            pltpu.make_async_copy(rows_ref.at[:, columns], held.at[:, columns], sems.at[at])
        )
        copies[-1].start()
    return copies


def place_columns(shift_ref, held, copies, placer, put):
    shift = jnp.transpose(jnp.broadcast_to(shift_ref[...].astype(jnp.float32), (LANES, ROWS)))
    shift = shift.astype(jnp.int32)
    lane = lax.broadcasted_iota(jnp.int32, (ROWS, LANES), 1)
    from_freq = lane % NF - shift
    valid = (from_freq >= 0) & (from_freq < NF)
    from_lane = jnp.where(valid, lane - shift, lane)
    for pair in range(TILES // 2):
        if pair % (TILES // 8) == 0:
            copies[pair // (TILES // 8)].wait()
        moved = []
        for tile in (2 * pair, 2 * pair + 1):
            block = held[:, tile * LANES : (tile + 1) * LANES].astype(jnp.float32)
            block = jnp.take_along_axis(block, from_lane, axis=1, mode="promise_in_bounds")
            moved.append(jnp.where(valid, block, 0.0).astype(jnp.bfloat16))
        placed = jnp.dot(
            placer, jnp.concatenate(moved, axis=1), preferred_element_type=jnp.float32
        )
        for half in range(2):
            put(2 * pair + half, placed[:, half * LANES : (half + 1) * LANES])


def send_out(wide, packed, out_ref, sem, size, parts):
    copies = []
    rows = size // parts
    for at in range(parts):
        part = pl.ds(at * rows, rows)
        packed[part, :] = wide[part, :].astype(jnp.bfloat16)
        copies.append(pltpu.make_async_copy(packed.at[part, :], out_ref.at[part, :], sem.at[at]))
        copies[-1].start()
    return copies


def place_kernel(
    target_ref, shift_ref, rows_ref, out_ref, held, wide, packed, in_sems, out_sems
):
    copies = fetch_rows(rows_ref, held, in_sems)
    _, member, _, count = row_slots(target_ref)
    placer = jnp.concatenate([one_hot(member & (count == k)) for k in range(CAP)], axis=0)

    def put(tile, placed):
        for k in range(CAP):
            wide[pl.ds(k * TILES + tile, DEVICES, stride=CHUNK), :] = placed[
                k * DEVICES : (k + 1) * DEVICES
            ]

    place_columns(shift_ref, held, copies, placer, put)
    codes = read_codes(placer, target_ref[...] % ROWS + 1)
    wide[pl.ds(LABELS, DEVICES, stride=CHUNK), :] = labels(
        *(codes[k * DEVICES : (k + 1) * DEVICES] for k in range(CAP))
    )
    for copy in send_out(wide, packed, out_ref, out_sems, DEVICES * CHUNK, 4):
        copy.wait()


def collect_kernel(
    where_ref, bubble_ref, box_ref, gamma_ref, w0, w1, w2, w3,
    box, wide, gamma_held, in_sems, out_sems,
):
    parts = 8
    rows = DEVICES * CHUNK // parts
    copies = []
    for at in range(parts):
        part = pl.ds(at * rows, rows)
        copies.append(
            pltpu.make_async_copy(box_ref.at[part, :], box.at[part, :], in_sems.at[at])
        )
        copies[-1].start()
    g, h, along_g, along_h = (where_ref[i] for i in range(4))
    for at in range(parts):
        copies[at].wait()
        part = pl.ds(at * rows, rows)
        wide[part, :] = box[part, :].astype(jnp.float32)
    label = jnp.transpose(wide[pl.ds(LABELS, DEVICES, stride=CHUNK), :]).astype(jnp.int32)
    row_of = lax.broadcasted_iota(jnp.int32, (ROWS, DEVICES), 0) + 1
    collector = jnp.concatenate([one_hot(row_of == label[k : k + 1]) for k in range(CAP)], axis=1)

    copies = []
    for d, w_ref in enumerate((w0, w1, w2, w3)):
        for o in range(SIDE):
            slab = ((g + o) % SIDE) * along_g + ((h + d) % SIDE) * along_h
            columns = pl.ds(pl.multiple_of(slab * ROWS, ROWS), ROWS)
            came = []
            for k in range(CAP):
                halves = [
                    wide[pl.ds(k * TILES + slab * 2 + half, DEVICES, stride=CHUNK), :]
                    for half in range(2)
                ]
                came.append(jnp.concatenate(halves, axis=1).astype(jnp.bfloat16))
            summed = jnp.dot(
                collector, jnp.concatenate(came, axis=0), preferred_element_type=jnp.float32
            )
            gamma = HUBBARD + summed
            at = d * SIDE + o
            gamma_held[at] = gamma
            copies.append(
                pltpu.make_async_copy(
                    gamma_held.at[at], gamma_ref.at[:, columns], out_sems.at[at]
                )
            )
            copies[-1].start()
            w_ref[o] = (gamma * bubble_ref[:, columns]).astype(jnp.bfloat16)
    for copy in copies:
        copy.wait()


def ladder_kernel(parts, a_ref, *refs):
    out_ref = refs[-1]
    total = jnp.dot(a_ref[0], refs[0][...], preferred_element_type=jnp.float32)
    far = jnp.concatenate([refs[2][...], refs[3][...]], axis=0)
    for o, block in ((1, refs[1][...]), (2, far), (3, refs[4][...])):
        total += jnp.dot(a_ref[o], block, preferred_element_type=jnp.float32)
    for other in refs[parts:-1]:
        total += other[...].astype(jnp.float32)
    out_ref[...] = total.astype(out_ref.dtype)


def part_ladder(weighted, full_parts, side, dtype, *others):
    steps = HALF // CUT

    def columns(rows, first):
        return pl.BlockSpec((rows, CUT), lambda n: (0, first + n))

    return pl.pallas_call(
        functools.partial(ladder_kernel, len(full_parts)),
        grid=(steps,),
        in_specs=[pl.BlockSpec((SIDE, ROWS, ROWS), lambda n: (0, 0, 0))]
        + [columns(part.shape[0], side * steps) for part in full_parts]
        + [columns(ROWS, 0) for _ in others],
        out_specs=columns(ROWS, 0),
        out_shape=jax.ShapeDtypeStruct((ROWS, HALF), dtype),
        compiler_params=pltpu.CompilerParams(vmem_limit_bytes=14 * MIB),
        cost_estimate=pl.CostEstimate(
            flops=2 * ROWS * 4 * ROWS * HALF, bytes_accessed=6 * MIB, transcendentals=0
        ),
        name="part_ladder",
    )(weighted, *full_parts, *others)


def join_kernel(*refs):
    left, right, out_ref = refs[-3:]
    out_ref[...] = left[...] + right[...].astype(jnp.float32)


def join(side, own, other, into=()):
    steps = HALF // CUT
    part = pl.BlockSpec((ROWS, CUT), lambda n: (0, n))
    return pl.pallas_call(
        join_kernel,
        grid=(steps,),
        in_specs=[pl.BlockSpec(memory_space=pl.ANY)] * len(into) + [part, part],
        out_specs=pl.BlockSpec((ROWS, CUT), lambda n: (0, side * steps + n)),
        out_shape=jax.ShapeDtypeStruct((ROWS, WIDTH), jnp.float32),
        input_output_aliases={0: 0} if into else {},
        compiler_params=pltpu.CompilerParams(vmem_limit_bytes=8 * MIB),
        cost_estimate=pl.CostEstimate(
            flops=ROWS * HALF, bytes_accessed=5 * MIB, transcendentals=0
        ),
        name="join",
    )(*into, own, other)


def per_device(vert_ph, full_pp, target, shift, trans_mom, trans_bose, energies, pair_table):
    tq = lax.axis_index("tq")
    slab = lax.axis_index("slab")
    core = tq % 2
    x, y = slab // SIDE, slab % SIDE
    g = jnp.where(core == 0, x, y)
    h = jnp.where(core == 0, y, x)
    along_g = jnp.where(core == 0, SIDE, 1)
    where = jnp.stack([g, h, along_g, SIDE + 1 - along_g]).astype(jnp.int32)

    full = full_pp.reshape(ROWS, WIDTH)
    left = move_g(full, 1)
    right = move_g(full, 3)
    far_top = move_g(left[: ROWS // 2], 1)
    far_low = move_g(right[ROWS // 2 :], 3)
    full_parts = (full, right, far_top, far_low, left)

    whole = pl.BlockSpec(memory_space=pltpu.VMEM)
    hbm = pl.BlockSpec(memory_space=pltpu.HBM)
    slots = (DEVICES * CHUNK, LANES)
    payload = pl.pallas_call(
        place_kernel,
        in_specs=[whole, whole, hbm],
        out_specs=hbm,
        out_shape=jax.ShapeDtypeStruct(slots, jnp.bfloat16),
        scratch_shapes=[
            pltpu.VMEM((ROWS, WIDTH), jnp.bfloat16),
            pltpu.VMEM(slots, jnp.float32),
            pltpu.VMEM(slots, jnp.bfloat16),
            pltpu.SemaphoreType.DMA((4,)),
            pltpu.SemaphoreType.DMA((4,)),
        ],
        compiler_params=pltpu.CompilerParams(vmem_limit_bytes=60 * MIB),
        cost_estimate=pl.CostEstimate(
            flops=2 * 384 * ROWS * WIDTH, bytes_accessed=5 * MIB, transcendentals=0
        ),
        name="place",
    )(target, shift, vert_ph.reshape(ROWS, WIDTH))
    arrived = lax.all_to_all(
        payload.reshape(DEVICES, CHUNK, LANES), AXES, split_axis=0, concat_axis=0, tiled=True
    ).reshape(DEVICES * CHUNK, LANES)


    scalar = pl.BlockSpec(memory_space=pltpu.SMEM)
    pair_bubble = pl.pallas_call(
        bubble_kernel,
        in_specs=[scalar, scalar, whole, whole],
        out_specs=whole,
        out_shape=jax.ShapeDtypeStruct((1, WIDTH), jnp.float32),
        compiler_params=pltpu.CompilerParams(vmem_limit_bytes=16 * MIB),
        cost_estimate=pl.CostEstimate(
            flops=10**11, bytes_accessed=1024 * MIB, transcendentals=0
        ),
        name="bubble",
    )(trans_mom, trans_bose, energies.reshape(1, NQ), pair_table)

    block = jax.ShapeDtypeStruct((SIDE, ROWS, ROWS), jnp.bfloat16)
    gamma, own, w1, w2, w3 = pl.pallas_call(
        collect_kernel,
        in_specs=[pl.BlockSpec(memory_space=pltpu.SMEM), whole, hbm],
        out_specs=[hbm] + [whole] * 4,
        out_shape=[jax.ShapeDtypeStruct((ROWS, WIDTH), jnp.float32)] + [block] * 4,
        scratch_shapes=[
            pltpu.VMEM(slots, jnp.bfloat16),
            pltpu.VMEM(slots, jnp.float32),
            pltpu.VMEM((SIDE * SIDE, ROWS, ROWS), jnp.float32),
            pltpu.SemaphoreType.DMA((8,)),
            pltpu.SemaphoreType.DMA((SIDE * SIDE,)),
        ],
        compiler_params=pltpu.CompilerParams(vmem_limit_bytes=24 * MIB),
        cost_estimate=pl.CostEstimate(
            flops=2 * 384 * ROWS * WIDTH, bytes_accessed=9 * MIB, transcendentals=0
        ),
        name="collect",
    )(where, pair_bubble, arrived)

    part = functools.partial(part_ladder, full_parts=full_parts)
    bf16, f32 = jnp.bfloat16, jnp.float32
    from_far, from_low, from_high = move_h(w2, 2), move_h(w1, 1), move_h(w3, 3)
    far_left = move_h(part(from_far, side=0, dtype=bf16), 1)
    from_far, from_low, from_high = lax.optimization_barrier((from_far, from_low, from_high))
    far_right = move_h(part(from_far, side=1, dtype=bf16), 3)
    high_right = move_h(part(from_high, side=1, dtype=bf16), 1)
    low_left = move_h(part(from_low, side=0, dtype=bf16), 3)
    high_left = move_h(part_ladder(from_high, full_parts, 0, bf16, far_left), 1)
    low_right = move_h(part_ladder(from_low, full_parts, 1, bf16, far_right), 3)
    own_left = part_ladder(own, full_parts, 0, f32, low_left)
    own_right = part_ladder(own, full_parts, 1, f32, high_right)
    ladder = join(0, own_left, high_left)
    ladder = join(1, own_right, low_right, (ladder,))
    return gamma[None], ladder[None]


def solution(mesh):
    in_specs = (
        P("tq", "slab", None),
        P("tq", "slab", None),
        P("tq", "slab"),
        P("tq", "slab"),
        P("tq"),
        P("tq"),
        P(),
        P(),
    )
    out_specs = (P("tq", "slab", None), P("tq", "slab", None))
    return jax.shard_map(
        per_device, mesh=mesh, in_specs=in_specs, out_specs=out_specs, check_vma=False
    )
```

```python
import functools

import jax
import jax.numpy as jnp
from jax import lax
from jax.experimental import pallas as pl
from jax.experimental.pallas import tpu as pltpu
from jax.sharding import PartitionSpec as P

NB = 32
NF = 64
NQ = 64

HUBBARD = 2.0
TEMPER = 0.25
PI_VALUE = 3.141592653589793

AXES = ("tq", "slab")
DEVICES = 128
CAP = 3
ROWS = 256
WIDTH = 4096
LANES = 128
TILES = WIDTH // LANES
LABELS = CAP * TILES
CHUNK = LABELS + 8
SIDE = 4
HALF = WIDTH // 2
CUT = 1024
MIB = 1024 * 1024


def bubble_kernel(mom_ref, bose_ref, energy_ref, table_ref, out_ref):
    exact = functools.partial(
        jnp.dot, precision=lax.Precision.HIGHEST, preferred_element_type=jnp.float32
    )
    energies = jnp.broadcast_to(energy_ref[...], (8, NQ))
    partner = table_ref[pl.ds(mom_ref[0], 1), :]
    picker = lax.broadcasted_iota(jnp.int32, (NQ, NQ), 0) == partner
    pair = exact(energies, picker.astype(jnp.float32))
    first = lax.broadcasted_iota(jnp.int32, (8, NQ), 0) == 0
    column = lax.broadcasted_iota(jnp.int32, (NQ, WIDTH), 1)
    spread = lax.broadcasted_iota(jnp.int32, (NQ, WIDTH), 0) == column // NF
    bands = exact(jnp.where(first, energies, pair), spread.astype(jnp.float32))
    band_own, band_pair = bands[:1], bands[1:2]
    freq = lax.broadcasted_iota(jnp.int32, (1, WIDTH), 1) % NF - NF // 2
    fermi = PI_VALUE * TEMPER * (2.0 * freq.astype(jnp.float32) + 1.0)
    bose = (bose_ref[0] - NB // 2).astype(jnp.float32) * (2.0 * PI_VALUE * TEMPER)
    other = bose - fermi
    top = TEMPER * (band_own * band_pair - fermi * other)
    below = (fermi * fermi + band_own * band_own) * (other * other + band_pair * band_pair)
    out_ref[...] = top / below


def pairs_along(axis_of_core, step):
    pairs = []
    for tq in range(8):
        axis = axis_of_core[tq % 2]
        for x in range(SIDE):
            for y in range(SIDE):
                to_x = (x + step) % SIDE if axis == 0 else x
                to_y = (y + step) % SIDE if axis == 1 else y
                pairs.append(((tq * SIDE + x) * SIDE + y, (tq * SIDE + to_x) * SIDE + to_y))
    return pairs


def move_g(array, step):
    return lax.ppermute(array, AXES, pairs_along((0, 1), step))


def move_h(array, step):
    return lax.ppermute(array, AXES, pairs_along((1, 0), step))


def one_hot(flags):
    return flags.astype(jnp.bfloat16)


def row_slots(target_ref):
    dest = target_ref[...] // ROWS
    member = lax.broadcasted_iota(jnp.int32, (DEVICES, ROWS), 0) == dest
    before = one_hot(
        lax.broadcasted_iota(jnp.int32, (ROWS, ROWS), 0)
        < lax.broadcasted_iota(jnp.int32, (ROWS, ROWS), 1)
    )
    count = jnp.dot(one_hot(member), before, preferred_element_type=jnp.float32)
    return dest, member, before, count


def read_codes(placer, values):
    return lax.dot_general(
        placer,
        jnp.broadcast_to(values, (LANES, ROWS)).astype(jnp.bfloat16),
        (((1,), (1,)), ((), ())),
        preferred_element_type=jnp.float32,
    )


def labels(*columns):
    rows = columns[0].shape[0]
    lane = lax.broadcasted_iota(jnp.int32, (rows, LANES), 1)
    label = jnp.zeros((rows, LANES), jnp.float32)
    for at, column in enumerate(columns):
        label = jnp.where(lane == at, column, label)
    return label


def fetch_rows(rows_ref, held, sems):
    quarter = WIDTH // 4
    copies = []
    for at in range(4):
        columns = pl.ds(at * quarter, quarter)
        copies.append(
            pltpu.make_async_copy(rows_ref.at[:, columns], held.at[:, columns], sems.at[at])
        )
        copies[-1].start()
    return copies


def place_columns(shift_ref, held, copies, placer, put):
    shift = jnp.transpose(jnp.broadcast_to(shift_ref[...].astype(jnp.float32), (LANES, ROWS)))
    shift = shift.astype(jnp.int32)
    lane = lax.broadcasted_iota(jnp.int32, (ROWS, LANES), 1)
    from_freq = lane % NF - shift
    valid = (from_freq >= 0) & (from_freq < NF)
    from_lane = jnp.where(valid, lane - shift, lane)
    for pair in range(TILES // 2):
        if pair % (TILES // 8) == 0:
            copies[pair // (TILES // 8)].wait()
        moved = []
        for tile in (2 * pair, 2 * pair + 1):
            block = held[:, tile * LANES : (tile + 1) * LANES].astype(jnp.float32)
            block = jnp.take_along_axis(block, from_lane, axis=1, mode="promise_in_bounds")
            moved.append(jnp.where(valid, block, 0.0).astype(jnp.bfloat16))
        placed = jnp.dot(
            placer, jnp.concatenate(moved, axis=1), preferred_element_type=jnp.float32
        )
        for half in range(2):
            put(2 * pair + half, placed[:, half * LANES : (half + 1) * LANES])


def send_out(wide, packed, out_ref, sem, size, parts):
    copies = []
    rows = size // parts
    for at in range(parts):
        part = pl.ds(at * rows, rows)
        packed[part, :] = wide[part, :].astype(jnp.bfloat16)
        copies.append(pltpu.make_async_copy(packed.at[part, :], out_ref.at[part, :], sem.at[at]))
        copies[-1].start()
    return copies


def place_kernel(
    target_ref, shift_ref, rows_ref, out_ref, held, wide, packed, in_sems, out_sems
):
    copies = fetch_rows(rows_ref, held, in_sems)
    _, member, _, count = row_slots(target_ref)
    placer = jnp.concatenate([one_hot(member & (count == k)) for k in range(CAP)], axis=0)

    def put(tile, placed):
        for k in range(CAP):
            wide[pl.ds(k * TILES + tile, DEVICES, stride=CHUNK), :] = placed[
                k * DEVICES : (k + 1) * DEVICES
            ]

    place_columns(shift_ref, held, copies, placer, put)
    codes = read_codes(placer, target_ref[...] % ROWS + 1)
    wide[pl.ds(LABELS, DEVICES, stride=CHUNK), :] = labels(
        *(codes[k * DEVICES : (k + 1) * DEVICES] for k in range(CAP))
    )
    for copy in send_out(wide, packed, out_ref, out_sems, DEVICES * CHUNK, 4):
        copy.wait()


def collect_kernel(turns, where_ref, bubble_ref, box_ref, *refs):
    gamma_ref, *w_refs, box, wide, gamma_held, in_sems, out_sems = refs[-6 - len(turns) :]
    parts = 8
    rows = DEVICES * CHUNK // parts
    copies = []
    for at in range(parts):
        part = pl.ds(at * rows, rows)
        copies.append(
            pltpu.make_async_copy(box_ref.at[part, :], box.at[part, :], in_sems.at[at])
        )
        copies[-1].start()
    g, h, along_g, along_h = (where_ref[i] for i in range(4))
    for at in range(parts):
        copies[at].wait()
        part = pl.ds(at * rows, rows)
        wide[part, :] = box[part, :].astype(jnp.float32)
    label = jnp.transpose(wide[pl.ds(LABELS, DEVICES, stride=CHUNK), :]).astype(jnp.int32)
    row_of = lax.broadcasted_iota(jnp.int32, (ROWS, DEVICES), 0) + 1
    collector = jnp.concatenate([one_hot(row_of == label[k : k + 1]) for k in range(CAP)], axis=1)

    copies = []
    for turn, (d, w_ref) in enumerate(zip(turns, w_refs)):
        for o in range(SIDE):
            slab = ((g + o) % SIDE) * along_g + ((h + d) % SIDE) * along_h
            columns = pl.ds(pl.multiple_of(slab * ROWS, ROWS), ROWS)
            came = []
            for k in range(CAP):
                halves = [
                    wide[pl.ds(k * TILES + slab * 2 + half, DEVICES, stride=CHUNK), :]
                    for half in range(2)
                ]
                came.append(jnp.concatenate(halves, axis=1).astype(jnp.bfloat16))
            summed = jnp.dot(
                collector, jnp.concatenate(came, axis=0), preferred_element_type=jnp.float32
            )
            gamma = HUBBARD + summed
            at = turn * SIDE + o
            gamma_held[at] = gamma
            copies.append(
                pltpu.make_async_copy(
                    gamma_held.at[at], gamma_ref.at[:, columns], out_sems.at[at]
                )
            )
            copies[-1].start()
            w_ref[o] = (gamma * bubble_ref[:, columns]).astype(jnp.bfloat16)
    for copy in copies:
        copy.wait()


def ladder_kernel(parts, a_ref, *refs):
    out_ref = refs[-1]
    total = jnp.dot(a_ref[0], refs[0][...], preferred_element_type=jnp.float32)
    far = jnp.concatenate([refs[2][...], refs[3][...]], axis=0)
    for o, block in ((1, refs[1][...]), (2, far), (3, refs[4][...])):
        total += jnp.dot(a_ref[o], block, preferred_element_type=jnp.float32)
    for other in refs[parts:-1]:
        total += other[...].astype(jnp.float32)
    out_ref[...] = total.astype(out_ref.dtype)


def part_ladder(weighted, full_parts, side, dtype, *others):
    steps = HALF // CUT

    def columns(rows, first):
        return pl.BlockSpec((rows, CUT), lambda n: (0, first + n))

    return pl.pallas_call(
        functools.partial(ladder_kernel, len(full_parts)),
        grid=(steps,),
        in_specs=[pl.BlockSpec((SIDE, ROWS, ROWS), lambda n: (0, 0, 0))]
        + [columns(part.shape[0], side * steps) for part in full_parts]
        + [columns(ROWS, 0) for _ in others],
        out_specs=columns(ROWS, 0),
        out_shape=jax.ShapeDtypeStruct((ROWS, HALF), dtype),
        compiler_params=pltpu.CompilerParams(vmem_limit_bytes=14 * MIB),
        cost_estimate=pl.CostEstimate(
            flops=2 * ROWS * 4 * ROWS * HALF, bytes_accessed=6 * MIB, transcendentals=0
        ),
        name="part_ladder",
    )(weighted, *full_parts, *others)


def join_kernel(*refs):
    left, right, out_ref = refs[-3:]
    out_ref[...] = left[...] + right[...].astype(jnp.float32)


def join(side, own, other, into=()):
    steps = HALF // CUT
    part = pl.BlockSpec((ROWS, CUT), lambda n: (0, n))
    return pl.pallas_call(
        join_kernel,
        grid=(steps,),
        in_specs=[pl.BlockSpec(memory_space=pl.ANY)] * len(into) + [part, part],
        out_specs=pl.BlockSpec((ROWS, CUT), lambda n: (0, side * steps + n)),
        out_shape=jax.ShapeDtypeStruct((ROWS, WIDTH), jnp.float32),
        input_output_aliases={0: 0} if into else {},
        compiler_params=pltpu.CompilerParams(vmem_limit_bytes=8 * MIB),
        cost_estimate=pl.CostEstimate(
            flops=ROWS * HALF, bytes_accessed=5 * MIB, transcendentals=0
        ),
        name="join",
    )(*into, own, other)


def per_device(vert_ph, full_pp, target, shift, trans_mom, trans_bose, energies, pair_table):
    tq = lax.axis_index("tq")
    slab = lax.axis_index("slab")
    core = tq % 2
    x, y = slab // SIDE, slab % SIDE
    g = jnp.where(core == 0, x, y)
    h = jnp.where(core == 0, y, x)
    along_g = jnp.where(core == 0, SIDE, 1)
    where = jnp.stack([g, h, along_g, SIDE + 1 - along_g]).astype(jnp.int32)

    full = full_pp.reshape(ROWS, WIDTH)
    left = move_g(full, 1)
    right = move_g(full, 3)
    far_top = move_g(left[: ROWS // 2], 1)
    far_low = move_g(right[ROWS // 2 :], 3)
    full_parts = (full, right, far_top, far_low, left)

    whole = pl.BlockSpec(memory_space=pltpu.VMEM)
    hbm = pl.BlockSpec(memory_space=pltpu.HBM)
    slots = (DEVICES * CHUNK, LANES)
    payload = pl.pallas_call(
        place_kernel,
        in_specs=[whole, whole, hbm],
        out_specs=hbm,
        out_shape=jax.ShapeDtypeStruct(slots, jnp.bfloat16),
        scratch_shapes=[
            pltpu.VMEM((ROWS, WIDTH), jnp.bfloat16),
            pltpu.VMEM(slots, jnp.float32),
            pltpu.VMEM(slots, jnp.bfloat16),
            pltpu.SemaphoreType.DMA((4,)),
            pltpu.SemaphoreType.DMA((4,)),
        ],
        compiler_params=pltpu.CompilerParams(vmem_limit_bytes=60 * MIB),
        cost_estimate=pl.CostEstimate(
            flops=2 * 384 * ROWS * WIDTH, bytes_accessed=5 * MIB, transcendentals=0
        ),
        name="place",
    )(target, shift, vert_ph.reshape(ROWS, WIDTH))
    arrived = lax.all_to_all(
        payload.reshape(DEVICES, CHUNK, LANES), AXES, split_axis=0, concat_axis=0, tiled=True
    ).reshape(DEVICES * CHUNK, LANES)


    scalar = pl.BlockSpec(memory_space=pltpu.SMEM)
    pair_bubble = pl.pallas_call(
        bubble_kernel,
        in_specs=[scalar, scalar, whole, whole],
        out_specs=whole,
        out_shape=jax.ShapeDtypeStruct((1, WIDTH), jnp.float32),
        compiler_params=pltpu.CompilerParams(vmem_limit_bytes=16 * MIB),
        cost_estimate=pl.CostEstimate(
            flops=10**11, bytes_accessed=1024 * MIB, transcendentals=0
        ),
        name="bubble",
    )(trans_mom, trans_bose, energies.reshape(1, NQ), pair_table)

    block = jax.ShapeDtypeStruct((SIDE, ROWS, ROWS), jnp.bfloat16)
    def collect(turns, *into):
        return pl.pallas_call(
            functools.partial(collect_kernel, turns),
            in_specs=[pl.BlockSpec(memory_space=pltpu.SMEM), whole, hbm] + [hbm] * len(into),
            out_specs=[hbm] + [whole] * len(turns),
            out_shape=[jax.ShapeDtypeStruct((ROWS, WIDTH), jnp.float32)] + [block] * len(turns),
            input_output_aliases={3: 0} if into else {},
            scratch_shapes=[
                pltpu.VMEM(slots, jnp.bfloat16),
                pltpu.VMEM(slots, jnp.float32),
                pltpu.VMEM((len(turns) * SIDE, ROWS, ROWS), jnp.float32),
                pltpu.SemaphoreType.DMA((8,)),
                pltpu.SemaphoreType.DMA((len(turns) * SIDE,)),
            ],
            compiler_params=pltpu.CompilerParams(vmem_limit_bytes=24 * MIB),
            cost_estimate=pl.CostEstimate(
                flops=2 * 384 * ROWS * WIDTH * len(turns) // SIDE,
                bytes_accessed=(4 + len(turns)) * MIB,
                transcendentals=0,
            ),
            name="collect",
        )(where, pair_bubble, arrived, *into)

    gamma, w2 = collect((2,))
    gamma, w1, w3, own = collect((1, 3, 0), gamma)

    part = functools.partial(part_ladder, full_parts=full_parts)
    bf16, f32 = jnp.bfloat16, jnp.float32
    from_far, from_low, from_high = move_h(w2, 2), move_h(w1, 1), move_h(w3, 3)
    far_left = move_h(part(from_far, side=0, dtype=bf16), 1)
    far_right = part(from_far, side=1, dtype=bf16)
    far_right, from_low, from_high = lax.optimization_barrier((far_right, from_low, from_high))
    far_right = move_h(far_right, 3)
    high_right = move_h(part(from_high, side=1, dtype=bf16), 1)
    low_left = move_h(part(from_low, side=0, dtype=bf16), 3)
    high_left = move_h(part_ladder(from_high, full_parts, 0, bf16, far_left), 1)
    low_right = move_h(part_ladder(from_low, full_parts, 1, bf16, far_right), 3)
    own_left = part_ladder(own, full_parts, 0, f32, low_left)
    own_right = part_ladder(own, full_parts, 1, f32, high_right)
    ladder = join(0, own_left, high_left)
    ladder = join(1, own_right, low_right, (ladder,))
    return gamma[None], ladder[None]


def solution(mesh):
    in_specs = (
        P("tq", "slab", None),
        P("tq", "slab", None),
        P("tq", "slab"),
        P("tq", "slab"),
        P("tq"),
        P("tq"),
        P(),
        P(),
    )
    out_specs = (P("tq", "slab", None), P("tq", "slab", None))
    return jax.shard_map(
        per_device, mesh=mesh, in_specs=in_specs, out_specs=out_specs, check_vma=False
    )
```

```python
import functools

import jax
import jax.numpy as jnp
from jax import lax
from jax.experimental import pallas as pl
from jax.experimental.pallas import tpu as pltpu
from jax.sharding import PartitionSpec as P

NB = 32
NF = 64
NQ = 64

HUBBARD = 2.0
TEMPER = 0.25
PI_VALUE = 3.141592653589793

AXES = ("tq", "slab")
DEVICES = 128
CAP = 3
ROWS = 256
WIDTH = 4096
LANES = 128
TILES = WIDTH // LANES
LABELS = CAP * TILES
CHUNK = LABELS + 8
SIDE = 4
HALF = WIDTH // 2
CUT = 1024
MIB = 1024 * 1024


def bubble_kernel(mom_ref, bose_ref, energy_ref, table_ref, out_ref):
    exact = functools.partial(
        jnp.dot, precision=lax.Precision.HIGHEST, preferred_element_type=jnp.float32
    )
    energies = jnp.broadcast_to(energy_ref[...], (8, NQ))
    partner = table_ref[pl.ds(mom_ref[0], 1), :]
    picker = lax.broadcasted_iota(jnp.int32, (NQ, NQ), 0) == partner
    pair = exact(energies, picker.astype(jnp.float32))
    first = lax.broadcasted_iota(jnp.int32, (8, NQ), 0) == 0
    column = lax.broadcasted_iota(jnp.int32, (NQ, WIDTH), 1)
    spread = lax.broadcasted_iota(jnp.int32, (NQ, WIDTH), 0) == column // NF
    bands = exact(jnp.where(first, energies, pair), spread.astype(jnp.float32))
    band_own, band_pair = bands[:1], bands[1:2]
    freq = lax.broadcasted_iota(jnp.int32, (1, WIDTH), 1) % NF - NF // 2
    fermi = PI_VALUE * TEMPER * (2.0 * freq.astype(jnp.float32) + 1.0)
    bose = (bose_ref[0] - NB // 2).astype(jnp.float32) * (2.0 * PI_VALUE * TEMPER)
    other = bose - fermi
    top = TEMPER * (band_own * band_pair - fermi * other)
    below = (fermi * fermi + band_own * band_own) * (other * other + band_pair * band_pair)
    out_ref[...] = top / below


def pairs_along(axis_of_core, step):
    pairs = []
    for tq in range(8):
        axis = axis_of_core[tq % 2]
        for x in range(SIDE):
            for y in range(SIDE):
                to_x = (x + step) % SIDE if axis == 0 else x
                to_y = (y + step) % SIDE if axis == 1 else y
                pairs.append(((tq * SIDE + x) * SIDE + y, (tq * SIDE + to_x) * SIDE + to_y))
    return pairs


def move_g(array, step):
    return lax.ppermute(array, AXES, pairs_along((0, 1), step))


def move_h(array, step):
    return lax.ppermute(array, AXES, pairs_along((1, 0), step))


def one_hot(flags):
    return flags.astype(jnp.bfloat16)


def row_slots(target_ref):
    dest = target_ref[...] // ROWS
    member = lax.broadcasted_iota(jnp.int32, (DEVICES, ROWS), 0) == dest
    before = one_hot(
        lax.broadcasted_iota(jnp.int32, (ROWS, ROWS), 0)
        < lax.broadcasted_iota(jnp.int32, (ROWS, ROWS), 1)
    )
    count = jnp.dot(one_hot(member), before, preferred_element_type=jnp.float32)
    return dest, member, before, count


def read_codes(placer, values):
    return lax.dot_general(
        placer,
        jnp.broadcast_to(values, (LANES, ROWS)).astype(jnp.bfloat16),
        (((1,), (1,)), ((), ())),
        preferred_element_type=jnp.float32,
    )


def labels(*columns):
    rows = columns[0].shape[0]
    lane = lax.broadcasted_iota(jnp.int32, (rows, LANES), 1)
    label = jnp.zeros((rows, LANES), jnp.float32)
    for at, column in enumerate(columns):
        label = jnp.where(lane == at, column, label)
    return label


def fetch_rows(rows_ref, held, sems):
    quarter = WIDTH // 4
    copies = []
    for at in range(4):
        columns = pl.ds(at * quarter, quarter)
        copies.append(
            pltpu.make_async_copy(rows_ref.at[:, columns], held.at[:, columns], sems.at[at])
        )
        copies[-1].start()
    return copies


def place_columns(shift_ref, held, copies, placer, put):
    shift = jnp.transpose(jnp.broadcast_to(shift_ref[...].astype(jnp.float32), (LANES, ROWS)))
    shift = shift.astype(jnp.int32)
    lane = lax.broadcasted_iota(jnp.int32, (ROWS, LANES), 1)
    from_freq = lane % NF - shift
    valid = (from_freq >= 0) & (from_freq < NF)
    from_lane = jnp.where(valid, lane - shift, lane)
    for pair in range(TILES // 2):
        if pair % (TILES // 8) == 0:
            copies[pair // (TILES // 8)].wait()
        moved = []
        for tile in (2 * pair, 2 * pair + 1):
            block = held[:, tile * LANES : (tile + 1) * LANES].astype(jnp.float32)
            block = jnp.take_along_axis(block, from_lane, axis=1, mode="promise_in_bounds")
            moved.append(jnp.where(valid, block, 0.0).astype(jnp.bfloat16))
        placed = jnp.dot(
            placer, jnp.concatenate(moved, axis=1), preferred_element_type=jnp.float32
        )
        for half in range(2):
            put(2 * pair + half, placed[:, half * LANES : (half + 1) * LANES])


def send_out(wide, packed, out_ref, sem, size, parts):
    copies = []
    rows = size // parts
    for at in range(parts):
        part = pl.ds(at * rows, rows)
        packed[part, :] = wide[part, :].astype(jnp.bfloat16)
        copies.append(pltpu.make_async_copy(packed.at[part, :], out_ref.at[part, :], sem.at[at]))
        copies[-1].start()
    return copies


def place_kernel(
    target_ref, shift_ref, rows_ref, out_ref, held, wide, packed, in_sems, out_sems
):
    copies = fetch_rows(rows_ref, held, in_sems)
    _, member, _, count = row_slots(target_ref)
    placer = jnp.concatenate([one_hot(member & (count == k)) for k in range(CAP)], axis=0)

    def put(tile, placed):
        for k in range(CAP):
            wide[pl.ds(k * TILES + tile, DEVICES, stride=CHUNK), :] = placed[
                k * DEVICES : (k + 1) * DEVICES
            ]

    place_columns(shift_ref, held, copies, placer, put)
    codes = read_codes(placer, target_ref[...] % ROWS + 1)
    wide[pl.ds(LABELS, DEVICES, stride=CHUNK), :] = labels(
        *(codes[k * DEVICES : (k + 1) * DEVICES] for k in range(CAP))
    )
    for copy in send_out(wide, packed, out_ref, out_sems, DEVICES * CHUNK, 4):
        copy.wait()


def collect_kernel(turns, where_ref, bubble_ref, box_ref, *refs):
    gamma_ref, *w_refs, box, wide, gamma_held, in_sems, out_sems = refs[-6 - len(turns) :]
    parts = 8
    rows = DEVICES * CHUNK // parts
    copies = []
    for at in range(parts):
        part = pl.ds(at * rows, rows)
        copies.append(
            pltpu.make_async_copy(box_ref.at[part, :], box.at[part, :], in_sems.at[at])
        )
        copies[-1].start()
    g, h, along_g, along_h = (where_ref[i] for i in range(4))
    for at in range(parts):
        copies[at].wait()
        part = pl.ds(at * rows, rows)
        wide[part, :] = box[part, :].astype(jnp.float32)
    label = jnp.transpose(wide[pl.ds(LABELS, DEVICES, stride=CHUNK), :]).astype(jnp.int32)
    row_of = lax.broadcasted_iota(jnp.int32, (ROWS, DEVICES), 0) + 1
    collector = jnp.concatenate([one_hot(row_of == label[k : k + 1]) for k in range(CAP)], axis=1)

    copies = []
    for turn, (d, w_ref) in enumerate(zip(turns, w_refs)):
        for o in range(SIDE):
            slab = ((g + o) % SIDE) * along_g + ((h + d) % SIDE) * along_h
            columns = pl.ds(pl.multiple_of(slab * ROWS, ROWS), ROWS)
            came = []
            for k in range(CAP):
                halves = [
                    wide[pl.ds(k * TILES + slab * 2 + half, DEVICES, stride=CHUNK), :]
                    for half in range(2)
                ]
                came.append(jnp.concatenate(halves, axis=1).astype(jnp.bfloat16))
            summed = jnp.dot(
                collector, jnp.concatenate(came, axis=0), preferred_element_type=jnp.float32
            )
            gamma = HUBBARD + summed
            at = turn * SIDE + o
            gamma_held[at] = gamma
            copies.append(
                pltpu.make_async_copy(
                    gamma_held.at[at], gamma_ref.at[:, columns], out_sems.at[at]
                )
            )
            copies[-1].start()
            w_ref[o] = (gamma * bubble_ref[:, columns]).astype(jnp.bfloat16)
    for copy in copies:
        copy.wait()


def ladder_kernel(parts, a_ref, *refs):
    out_ref = refs[-1]
    total = jnp.dot(a_ref[0], refs[0][...], preferred_element_type=jnp.float32)
    far = jnp.concatenate([refs[2][...], refs[3][...]], axis=0)
    for o, block in ((1, refs[1][...]), (2, far), (3, refs[4][...])):
        total += jnp.dot(a_ref[o], block, preferred_element_type=jnp.float32)
    for other in refs[parts:-1]:
        total += other[...].astype(jnp.float32)
    out_ref[...] = total.astype(out_ref.dtype)


def part_ladder(weighted, full_parts, side, dtype, *others):
    steps = HALF // CUT

    def columns(rows, first):
        return pl.BlockSpec((rows, CUT), lambda n: (0, first + n))

    return pl.pallas_call(
        functools.partial(ladder_kernel, len(full_parts)),
        grid=(steps,),
        in_specs=[pl.BlockSpec((SIDE, ROWS, ROWS), lambda n: (0, 0, 0))]
        + [columns(part.shape[0], side * steps) for part in full_parts]
        + [columns(ROWS, 0) for _ in others],
        out_specs=columns(ROWS, 0),
        out_shape=jax.ShapeDtypeStruct((ROWS, HALF), dtype),
        compiler_params=pltpu.CompilerParams(vmem_limit_bytes=14 * MIB),
        cost_estimate=pl.CostEstimate(
            flops=2 * ROWS * 4 * ROWS * HALF, bytes_accessed=6 * MIB, transcendentals=0
        ),
        name="part_ladder",
    )(weighted, *full_parts, *others)


def join_kernel(*refs):
    left, right, out_ref = refs[-3:]
    out_ref[...] = left[...] + right[...].astype(jnp.float32)


def join(side, own, other, into=()):
    steps = HALF // CUT
    part = pl.BlockSpec((ROWS, CUT), lambda n: (0, n))
    return pl.pallas_call(
        join_kernel,
        grid=(steps,),
        in_specs=[pl.BlockSpec(memory_space=pl.ANY)] * len(into) + [part, part],
        out_specs=pl.BlockSpec((ROWS, CUT), lambda n: (0, side * steps + n)),
        out_shape=jax.ShapeDtypeStruct((ROWS, WIDTH), jnp.float32),
        input_output_aliases={0: 0} if into else {},
        compiler_params=pltpu.CompilerParams(vmem_limit_bytes=8 * MIB),
        cost_estimate=pl.CostEstimate(
            flops=ROWS * HALF, bytes_accessed=5 * MIB, transcendentals=0
        ),
        name="join",
    )(*into, own, other)


def per_device(vert_ph, full_pp, target, shift, trans_mom, trans_bose, energies, pair_table):
    tq = lax.axis_index("tq")
    slab = lax.axis_index("slab")
    core = tq % 2
    x, y = slab // SIDE, slab % SIDE
    g = jnp.where(core == 0, x, y)
    h = jnp.where(core == 0, y, x)
    along_g = jnp.where(core == 0, SIDE, 1)
    where = jnp.stack([g, h, along_g, SIDE + 1 - along_g]).astype(jnp.int32)

    full = full_pp.reshape(ROWS, WIDTH)
    left = move_g(full, 1)
    right = move_g(full, 3)
    far_top = move_g(left[: ROWS // 2], 1)
    far_low = move_g(right[ROWS // 2 :], 3)
    full_parts = (full, right, far_top, far_low, left)

    whole = pl.BlockSpec(memory_space=pltpu.VMEM)
    hbm = pl.BlockSpec(memory_space=pltpu.HBM)
    slots = (DEVICES * CHUNK, LANES)
    spread = ((DEVICES + 1) * CHUNK, LANES)
    payload = pl.pallas_call(
        place_kernel,
        in_specs=[whole, whole, hbm],
        out_specs=hbm,
        out_shape=jax.ShapeDtypeStruct(slots, jnp.bfloat16),
        scratch_shapes=[
            pltpu.VMEM((ROWS, WIDTH), jnp.bfloat16),
            pltpu.VMEM(spread, jnp.float32),
            pltpu.VMEM(slots, jnp.bfloat16),
            pltpu.SemaphoreType.DMA((4,)),
            pltpu.SemaphoreType.DMA((4,)),
        ],
        compiler_params=pltpu.CompilerParams(vmem_limit_bytes=60 * MIB),
        cost_estimate=pl.CostEstimate(
            flops=2 * 384 * ROWS * WIDTH, bytes_accessed=5 * MIB, transcendentals=0
        ),
        name="place",
    )(target, shift, vert_ph.reshape(ROWS, WIDTH))
    arrived = lax.all_to_all(
        payload.reshape(DEVICES, CHUNK, LANES), AXES, split_axis=0, concat_axis=0, tiled=True
    ).reshape(DEVICES * CHUNK, LANES)


    scalar = pl.BlockSpec(memory_space=pltpu.SMEM)
    pair_bubble = pl.pallas_call(
        bubble_kernel,
        in_specs=[scalar, scalar, whole, whole],
        out_specs=whole,
        out_shape=jax.ShapeDtypeStruct((1, WIDTH), jnp.float32),
        compiler_params=pltpu.CompilerParams(vmem_limit_bytes=16 * MIB),
        cost_estimate=pl.CostEstimate(
            flops=10**11, bytes_accessed=1024 * MIB, transcendentals=0
        ),
        name="bubble",
    )(trans_mom, trans_bose, energies.reshape(1, NQ), pair_table)

    block = jax.ShapeDtypeStruct((SIDE, ROWS, ROWS), jnp.bfloat16)
    def collect(turns, *into):
        return pl.pallas_call(
            functools.partial(collect_kernel, turns),
            in_specs=[pl.BlockSpec(memory_space=pltpu.SMEM), whole, hbm] + [hbm] * len(into),
            out_specs=[hbm] + [whole] * len(turns),
            out_shape=[jax.ShapeDtypeStruct((ROWS, WIDTH), jnp.float32)] + [block] * len(turns),
            input_output_aliases={3: 0} if into else {},
            scratch_shapes=[
                pltpu.VMEM(slots, jnp.bfloat16),
                pltpu.VMEM(spread, jnp.float32),
                pltpu.VMEM((len(turns) * SIDE, ROWS, ROWS), jnp.float32),
                pltpu.SemaphoreType.DMA((8,)),
                pltpu.SemaphoreType.DMA((len(turns) * SIDE,)),
            ],
            compiler_params=pltpu.CompilerParams(vmem_limit_bytes=24 * MIB),
            cost_estimate=pl.CostEstimate(
                flops=2 * 384 * ROWS * WIDTH * len(turns) // SIDE,
                bytes_accessed=(4 + len(turns)) * MIB,
                transcendentals=0,
            ),
            name="collect",
        )(where, pair_bubble, arrived, *into)

    gamma, w2 = collect((2,))
    gamma, w1, w3, own = collect((1, 3, 0), gamma)

    part = functools.partial(part_ladder, full_parts=full_parts)
    bf16, f32 = jnp.bfloat16, jnp.float32
    from_far, from_low, from_high = move_h(w2, 2), move_h(w1, 1), move_h(w3, 3)
    far_left = move_h(part(from_far, side=0, dtype=bf16), 1)
    far_right = part(from_far, side=1, dtype=bf16)
    far_right, from_low, from_high = lax.optimization_barrier((far_right, from_low, from_high))
    far_right = move_h(far_right, 3)
    high_right = move_h(part(from_high, side=1, dtype=bf16), 1)
    low_left = move_h(part(from_low, side=0, dtype=bf16), 3)
    high_left = move_h(part_ladder(from_high, full_parts, 0, bf16, far_left), 1)
    low_right = move_h(part_ladder(from_low, full_parts, 1, bf16, far_right), 3)
    own_left = part_ladder(own, full_parts, 0, f32, low_left)
    own_right = part_ladder(own, full_parts, 1, f32, high_right)
    ladder = join(0, own_left, high_left)
    ladder = join(1, own_right, low_right, (ladder,))
    return gamma[None], ladder[None]


def solution(mesh):
    in_specs = (
        P("tq", "slab", None),
        P("tq", "slab", None),
        P("tq", "slab"),
        P("tq", "slab"),
        P("tq"),
        P("tq"),
        P(),
        P(),
    )
    out_specs = (P("tq", "slab", None), P("tq", "slab", None))
    return jax.shard_map(
        per_device, mesh=mesh, in_specs=in_specs, out_specs=out_specs, check_vma=False
    )
```

```python
import functools

import jax
import jax.numpy as jnp
from jax import lax
from jax.experimental import pallas as pl
from jax.experimental.pallas import tpu as pltpu
from jax.sharding import PartitionSpec as P

NB = 32
NF = 64
NQ = 64

HUBBARD = 2.0
TEMPER = 0.25
PI_VALUE = 3.141592653589793

AXES = ("tq", "slab")
DEVICES = 128
CAP = 3
ROWS = 256
WIDTH = 4096
LANES = 128
TILES = WIDTH // LANES
LABELS = CAP * TILES
CHUNK = LABELS + 8
SIDE = 4
HALF = WIDTH // 2
CUT = 1024
MIB = 1024 * 1024


def bubble_kernel(mom_ref, bose_ref, energy_ref, table_ref, out_ref):
    exact = functools.partial(
        jnp.dot, precision=lax.Precision.HIGHEST, preferred_element_type=jnp.float32
    )
    energies = jnp.broadcast_to(energy_ref[...], (8, NQ))
    partner = table_ref[pl.ds(mom_ref[0], 1), :]
    picker = lax.broadcasted_iota(jnp.int32, (NQ, NQ), 0) == partner
    pair = exact(energies, picker.astype(jnp.float32))
    first = lax.broadcasted_iota(jnp.int32, (8, NQ), 0) == 0
    column = lax.broadcasted_iota(jnp.int32, (NQ, WIDTH), 1)
    spread = lax.broadcasted_iota(jnp.int32, (NQ, WIDTH), 0) == column // NF
    bands = exact(jnp.where(first, energies, pair), spread.astype(jnp.float32))
    band_own, band_pair = bands[:1], bands[1:2]
    freq = lax.broadcasted_iota(jnp.int32, (1, WIDTH), 1) % NF - NF // 2
    fermi = PI_VALUE * TEMPER * (2.0 * freq.astype(jnp.float32) + 1.0)
    bose = (bose_ref[0] - NB // 2).astype(jnp.float32) * (2.0 * PI_VALUE * TEMPER)
    other = bose - fermi
    top = TEMPER * (band_own * band_pair - fermi * other)
    below = (fermi * fermi + band_own * band_own) * (other * other + band_pair * band_pair)
    out_ref[...] = top / below


def pairs_along(axis_of_core, step):
    pairs = []
    for tq in range(8):
        axis = axis_of_core[tq % 2]
        for x in range(SIDE):
            for y in range(SIDE):
                to_x = (x + step) % SIDE if axis == 0 else x
                to_y = (y + step) % SIDE if axis == 1 else y
                pairs.append(((tq * SIDE + x) * SIDE + y, (tq * SIDE + to_x) * SIDE + to_y))
    return pairs


def move_g(array, step):
    return lax.ppermute(array, AXES, pairs_along((0, 1), step))


def move_h(array, step):
    return lax.ppermute(array, AXES, pairs_along((1, 0), step))


def one_hot(flags):
    return flags.astype(jnp.bfloat16)


def row_slots(target_ref):
    dest = target_ref[...] // ROWS
    member = lax.broadcasted_iota(jnp.int32, (DEVICES, ROWS), 0) == dest
    before = one_hot(
        lax.broadcasted_iota(jnp.int32, (ROWS, ROWS), 0)
        < lax.broadcasted_iota(jnp.int32, (ROWS, ROWS), 1)
    )
    count = jnp.dot(one_hot(member), before, preferred_element_type=jnp.float32)
    return dest, member, before, count


def read_codes(placer, values):
    return lax.dot_general(
        placer,
        jnp.broadcast_to(values, (LANES, ROWS)).astype(jnp.bfloat16),
        (((1,), (1,)), ((), ())),
        preferred_element_type=jnp.float32,
    )


def labels(*columns):
    rows = columns[0].shape[0]
    lane = lax.broadcasted_iota(jnp.int32, (rows, LANES), 1)
    label = jnp.zeros((rows, LANES), jnp.float32)
    for at, column in enumerate(columns):
        label = jnp.where(lane == at, column, label)
    return label


def fetch_rows(rows_ref, held, sems):
    quarter = WIDTH // 4
    copies = []
    for at in range(4):
        columns = pl.ds(at * quarter, quarter)
        copies.append(
            pltpu.make_async_copy(rows_ref.at[:, columns], held.at[:, columns], sems.at[at])
        )
        copies[-1].start()
    return copies


def place_columns(shift_ref, held, copies, placer, put):
    shift = jnp.transpose(jnp.broadcast_to(shift_ref[...].astype(jnp.float32), (LANES, ROWS)))
    shift = shift.astype(jnp.int32)
    lane = lax.broadcasted_iota(jnp.int32, (ROWS, LANES), 1)
    from_freq = lane % NF - shift
    valid = (from_freq >= 0) & (from_freq < NF)
    from_lane = jnp.where(valid, lane - shift, lane)
    for pair in range(TILES // 2):
        if pair % (TILES // 8) == 0:
            copies[pair // (TILES // 8)].wait()
        moved = []
        for tile in (2 * pair, 2 * pair + 1):
            block = held[:, tile * LANES : (tile + 1) * LANES].astype(jnp.float32)
            block = jnp.take_along_axis(block, from_lane, axis=1, mode="promise_in_bounds")
            moved.append(jnp.where(valid, block, 0.0).astype(jnp.bfloat16))
        placed = jnp.dot(
            placer, jnp.concatenate(moved, axis=1), preferred_element_type=jnp.float32
        )
        for half in range(2):
            put(2 * pair + half, placed[:, half * LANES : (half + 1) * LANES])


def send_out(wide, packed, out_ref, sem, size, parts):
    copies = []
    rows = size // parts
    for at in range(parts):
        part = pl.ds(at * rows, rows)
        packed[part, :] = wide[part, :].astype(jnp.bfloat16)
        copies.append(pltpu.make_async_copy(packed.at[part, :], out_ref.at[part, :], sem.at[at]))
        copies[-1].start()
    return copies


def place_kernel(
    target_ref, shift_ref, rows_ref, out_ref, held, wide, packed, in_sems, out_sems
):
    copies = fetch_rows(rows_ref, held, in_sems)
    _, member, _, count = row_slots(target_ref)
    placer = jnp.concatenate([one_hot(member & (count == k)) for k in range(CAP)], axis=0)

    def put(tile, placed):
        for k in range(CAP):
            wide[pl.ds(k * TILES + tile, DEVICES, stride=CHUNK), :] = placed[
                k * DEVICES : (k + 1) * DEVICES
            ]

    place_columns(shift_ref, held, copies, placer, put)
    codes = read_codes(placer, target_ref[...] % ROWS + 1)
    wide[pl.ds(LABELS, DEVICES, stride=CHUNK), :] = labels(
        *(codes[k * DEVICES : (k + 1) * DEVICES] for k in range(CAP))
    )
    for copy in send_out(wide, packed, out_ref, out_sems, DEVICES * CHUNK, 4):
        copy.wait()


def collect_kernel(turns, where_ref, bubble_ref, box_ref, *refs):
    gamma_ref, *w_refs, box, wide, gamma_held, in_sems, out_sems = refs[-6 - len(turns) :]
    parts = 8
    rows = DEVICES * CHUNK // parts
    copies = []
    for at in range(parts):
        part = pl.ds(at * rows, rows)
        copies.append(
            pltpu.make_async_copy(box_ref.at[part, :], box.at[part, :], in_sems.at[at])
        )
        copies[-1].start()
    g, h, along_g, along_h = (where_ref[i] for i in range(4))
    for at in range(parts):
        copies[at].wait()
        part = pl.ds(at * rows, rows)
        wide[part, :] = box[part, :].astype(jnp.float32)
    label = jnp.transpose(wide[pl.ds(LABELS, DEVICES, stride=CHUNK), :]).astype(jnp.int32)
    row_of = lax.broadcasted_iota(jnp.int32, (ROWS, DEVICES), 0) + 1
    collector = jnp.concatenate([one_hot(row_of == label[k : k + 1]) for k in range(CAP)], axis=1)

    copies = []
    for turn, (d, w_ref) in enumerate(zip(turns, w_refs)):
        for o in range(SIDE):
            slab = ((g + o) % SIDE) * along_g + ((h + d) % SIDE) * along_h
            columns = pl.ds(pl.multiple_of(slab * ROWS, ROWS), ROWS)
            came = []
            for k in range(CAP):
                halves = [
                    wide[pl.ds(k * TILES + slab * 2 + half, DEVICES, stride=CHUNK), :]
                    for half in range(2)
                ]
                came.append(jnp.concatenate(halves, axis=1).astype(jnp.bfloat16))
            summed = jnp.dot(
                collector, jnp.concatenate(came, axis=0), preferred_element_type=jnp.float32
            )
            gamma = HUBBARD + summed
            at = turn * SIDE + o
            gamma_held[at] = gamma
            copies.append(
                pltpu.make_async_copy(
                    gamma_held.at[at], gamma_ref.at[:, columns], out_sems.at[at]
                )
            )
            copies[-1].start()
            w_ref[o] = (gamma * bubble_ref[:, columns]).astype(jnp.bfloat16)
    for copy in copies:
        copy.wait()


def ladder_kernel(parts, a_ref, *refs):
    out_ref = refs[-1]
    total = jnp.dot(a_ref[0], refs[0][...], preferred_element_type=jnp.float32)
    far = jnp.concatenate([refs[2][...], refs[3][...]], axis=0)
    for o, block in ((1, refs[1][...]), (2, far), (3, refs[4][...])):
        total += jnp.dot(a_ref[o], block, preferred_element_type=jnp.float32)
    for other in refs[parts:-1]:
        total += other[...].astype(jnp.float32)
    out_ref[...] = total.astype(out_ref.dtype)


def part_ladder(weighted, full_parts, side, dtype, *others):
    steps = HALF // CUT

    def columns(rows, first):
        return pl.BlockSpec((rows, CUT), lambda n: (0, first + n))

    return pl.pallas_call(
        functools.partial(ladder_kernel, len(full_parts)),
        grid=(steps,),
        in_specs=[pl.BlockSpec((SIDE, ROWS, ROWS), lambda n: (0, 0, 0))]
        + [columns(part.shape[0], side * steps) for part in full_parts]
        + [columns(ROWS, 0) for _ in others],
        out_specs=columns(ROWS, 0),
        out_shape=jax.ShapeDtypeStruct((ROWS, HALF), dtype),
        compiler_params=pltpu.CompilerParams(vmem_limit_bytes=14 * MIB),
        cost_estimate=pl.CostEstimate(
            flops=2 * ROWS * 4 * ROWS * HALF, bytes_accessed=6 * MIB, transcendentals=0
        ),
        name="part_ladder",
    )(weighted, *full_parts, *others)


def join_kernel(*refs):
    left, right, out_ref = refs[-3:]
    out_ref[...] = left[...] + right[...].astype(jnp.float32)


def join(side, own, other, into=()):
    part = pl.BlockSpec((ROWS // 2, HALF), lambda n: (n, 0))
    return pl.pallas_call(
        join_kernel,
        grid=(2,),
        in_specs=[pl.BlockSpec(memory_space=pl.ANY)] * len(into) + [part, part],
        out_specs=pl.BlockSpec((ROWS // 2, HALF), lambda n: (n, side)),
        out_shape=jax.ShapeDtypeStruct((ROWS, WIDTH), jnp.float32),
        input_output_aliases={0: 0} if into else {},
        compiler_params=pltpu.CompilerParams(vmem_limit_bytes=8 * MIB),
        cost_estimate=pl.CostEstimate(
            flops=ROWS * HALF, bytes_accessed=5 * MIB, transcendentals=0
        ),
        name="join",
    )(*into, own, other)


def per_device(vert_ph, full_pp, target, shift, trans_mom, trans_bose, energies, pair_table):
    tq = lax.axis_index("tq")
    slab = lax.axis_index("slab")
    core = tq % 2
    x, y = slab // SIDE, slab % SIDE
    g = jnp.where(core == 0, x, y)
    h = jnp.where(core == 0, y, x)
    along_g = jnp.where(core == 0, SIDE, 1)
    where = jnp.stack([g, h, along_g, SIDE + 1 - along_g]).astype(jnp.int32)

    full = full_pp.reshape(ROWS, WIDTH)
    left = move_g(full, 1)
    right = move_g(full, 3)
    far_top = move_g(left[: ROWS // 2], 1)
    far_low = move_g(right[ROWS // 2 :], 3)
    full_parts = (full, right, far_top, far_low, left)

    whole = pl.BlockSpec(memory_space=pltpu.VMEM)
    hbm = pl.BlockSpec(memory_space=pltpu.HBM)
    slots = (DEVICES * CHUNK, LANES)
    spread = ((DEVICES + 1) * CHUNK, LANES)
    payload = pl.pallas_call(
        place_kernel,
        in_specs=[whole, whole, hbm],
        out_specs=hbm,
        out_shape=jax.ShapeDtypeStruct(slots, jnp.bfloat16),
        scratch_shapes=[
            pltpu.VMEM((ROWS, WIDTH), jnp.bfloat16),
            pltpu.VMEM(spread, jnp.float32),
            pltpu.VMEM(slots, jnp.bfloat16),
            pltpu.SemaphoreType.DMA((4,)),
            pltpu.SemaphoreType.DMA((4,)),
        ],
        compiler_params=pltpu.CompilerParams(vmem_limit_bytes=60 * MIB),
        cost_estimate=pl.CostEstimate(
            flops=2 * 384 * ROWS * WIDTH, bytes_accessed=5 * MIB, transcendentals=0
        ),
        name="place",
    )(target, shift, vert_ph.reshape(ROWS, WIDTH))
    arrived = lax.all_to_all(
        payload.reshape(DEVICES, CHUNK, LANES), AXES, split_axis=0, concat_axis=0, tiled=True
    ).reshape(DEVICES * CHUNK, LANES)


    scalar = pl.BlockSpec(memory_space=pltpu.SMEM)
    pair_bubble = pl.pallas_call(
        bubble_kernel,
        in_specs=[scalar, scalar, whole, whole],
        out_specs=whole,
        out_shape=jax.ShapeDtypeStruct((1, WIDTH), jnp.float32),
        compiler_params=pltpu.CompilerParams(vmem_limit_bytes=16 * MIB),
        cost_estimate=pl.CostEstimate(
            flops=10**11, bytes_accessed=1024 * MIB, transcendentals=0
        ),
        name="bubble",
    )(trans_mom, trans_bose, energies.reshape(1, NQ), pair_table)

    block = jax.ShapeDtypeStruct((SIDE, ROWS, ROWS), jnp.bfloat16)
    def collect(turns, *into):
        return pl.pallas_call(
            functools.partial(collect_kernel, turns),
            in_specs=[pl.BlockSpec(memory_space=pltpu.SMEM), whole, hbm] + [hbm] * len(into),
            out_specs=[hbm] + [whole] * len(turns),
            out_shape=[jax.ShapeDtypeStruct((ROWS, WIDTH), jnp.float32)] + [block] * len(turns),
            input_output_aliases={3: 0} if into else {},
            scratch_shapes=[
                pltpu.VMEM(slots, jnp.bfloat16),
                pltpu.VMEM(spread, jnp.float32),
                pltpu.VMEM((len(turns) * SIDE, ROWS, ROWS), jnp.float32),
                pltpu.SemaphoreType.DMA((8,)),
                pltpu.SemaphoreType.DMA((len(turns) * SIDE,)),
            ],
            compiler_params=pltpu.CompilerParams(vmem_limit_bytes=24 * MIB),
            cost_estimate=pl.CostEstimate(
                flops=2 * 384 * ROWS * WIDTH * len(turns) // SIDE,
                bytes_accessed=(4 + len(turns)) * MIB,
                transcendentals=0,
            ),
            name="collect",
        )(where, pair_bubble, arrived, *into)

    gamma, w2 = collect((2,))
    gamma, w1, w3 = collect((1, 3), gamma)
    gamma, own = collect((0,), gamma)

    part = functools.partial(part_ladder, full_parts=full_parts)
    bf16, f32 = jnp.bfloat16, jnp.float32
    from_far, from_low, from_high = move_h(w2, 2), move_h(w1, 1), move_h(w3, 3)
    far_left = move_h(part(from_far, side=0, dtype=bf16), 1)
    far_right = part(from_far, side=1, dtype=bf16)
    far_right, from_low, from_high = lax.optimization_barrier((far_right, from_low, from_high))
    far_right = move_h(far_right, 3)
    high_right = move_h(part(from_high, side=1, dtype=bf16), 1)
    low_left = move_h(part(from_low, side=0, dtype=bf16), 3)
    high_left = move_h(part_ladder(from_high, full_parts, 0, bf16, far_left), 1)
    low_right = move_h(part_ladder(from_low, full_parts, 1, bf16, far_right), 3)
    own_left = part_ladder(own, full_parts, 0, f32, low_left)
    own_right = part_ladder(own, full_parts, 1, f32, high_right)
    ladder = join(0, own_left, high_left)
    ladder = join(1, own_right, low_right, (ladder,))
    return gamma[None], ladder[None]


def solution(mesh):
    in_specs = (
        P("tq", "slab", None),
        P("tq", "slab", None),
        P("tq", "slab"),
        P("tq", "slab"),
        P("tq"),
        P("tq"),
        P(),
        P(),
    )
    out_specs = (P("tq", "slab", None), P("tq", "slab", None))
    return jax.shard_map(
        per_device, mesh=mesh, in_specs=in_specs, out_specs=out_specs, check_vma=False
    )
```
